128 devices in a mesh: cfg: 2 (over core), seq: 16 (over z, y), batch: 4 (over x).
Axes of the slice: x: 4, y: 4, z: 4, core: 2. Of those that a mesh axis runs over, the one named last changes fastest.
Arguments:
- queries: bfloat16 [2, 49152, 2048], P('cfg', ('batch', 'seq')), parts along dimension 1, may hold values from -6 to 6
- keys: bfloat16 [2, 49152, 2048], P('cfg', ('batch', 'seq')), parts along dimension 1, may hold values from -6 to 6
- values: bfloat16 [2, 49152, 2048], P('cfg', ('batch', 'seq')), parts along dimension 1, may hold values from -6 to 6
- neighbours: int32 [768, 11], P('batch'), parts along dimension 0, may hold values from 0 to 191, as said below
- w_out: bfloat16 [2048, 4096], replicated, may hold values from -0.125 to 0.125
Outputs:
- guided: bfloat16 [49152, 4096], P(('batch', 'seq'), 'cfg'), parts along dimension 0
The draws below stay inside these ranges and needn't reach their ends.
There are 4 independent parts, one for each index of `batch`. The reference program is written for one: setup_inputs(seed, part) draws one part's arguments, and reference() takes and returns one part's arrays. A program takes and returns all parts, laid end to end along the dimension named above; an argument that names none is the same for every part. Nothing has to cross between parts.
Inputs may be any that keep to these rules, and one draw needn't show every extreme that they name: `neighbours`: row t lists tile t itself first, then tiles of the same camera around it, then one tile of each of the two cameras beside it on the camera cycle.
All inputs are finite; a program needn't handle non-finite values.
Results may differ from the reference program's by a relative error of at most 0.0058.
Values may be sent and summed in bfloat16 or wider, within the bound.
A program may use at most 192 MiB of HBM per device.

```python
import jax
import jax.numpy as jnp
from jax import lax

D = 4096
HEADS = 16
HD = 128
TILE = 64
CAMS = 6
COLS = 4
NB = 11
E = 2048
TOKENS = 12288
TILES = 192
TILES_CAM = 32


def draw_queries(key, part):
    key = jax.random.fold_in(key, 1)
    return jnp.clip(jax.random.normal(key, (2, TOKENS, E)), -6.0, 6.0).astype(jnp.bfloat16)


def draw_keys(key, part):
    key = jax.random.fold_in(key, 2)
    return jnp.clip(jax.random.normal(key, (2, TOKENS, E)), -6.0, 6.0).astype(jnp.bfloat16)


def draw_neighbours(key, part):
    key = jax.random.fold_in(key, 3)
    cycle_order = jax.random.permutation(key, CAMS).astype(jnp.int32)
    cycle_place = jnp.argsort(cycle_order).astype(jnp.int32)
    tile_index = jnp.arange(TILES, dtype=jnp.int32)
    camera = tile_index // TILES_CAM
    local_tile = tile_index % TILES_CAM
    grid_rows = TILES_CAM // COLS
    tile_row = local_tile // COLS
    tile_col = local_tile % COLS
    columns = []
    for step_row in (0, -1, 1):
        for step_col in (0, -1, 1):
            if step_row == 0 and step_col == 0 and (len(columns) > 0):
                continue
            columns.append(camera * TILES_CAM + (tile_row + step_row) % grid_rows * COLS + (tile_col + step_col) % COLS)
    place_here = cycle_place[camera]
    left_camera = cycle_order[(place_here - 1) % CAMS]
    right_camera = cycle_order[(place_here + 1) % CAMS]
    columns.append(left_camera * TILES_CAM + tile_row * COLS + COLS - 1)
    columns.append(right_camera * TILES_CAM + tile_row * COLS)
    return jnp.stack(columns, axis=1).astype(jnp.int32)


def block_levels(rng, extent, pieces, least, top_value):
    loudness, own = 1.0, jax.random.fold_in(rng, 6)
    for axis_at, blocks in pieces:
        steps = jnp.exp(jax.random.uniform(jax.random.fold_in(own, axis_at), (blocks,), jnp.float32, least / len(pieces), top_value / len(pieces)))
        loudness = loudness * jnp.repeat(steps, extent[axis_at] // blocks).reshape([-1 if axis == axis_at else 1 for axis in range(len(extent))])
    return loudness


def gaussian(own_key, dims, deviation, most, cuts=(), held_as=jnp.bfloat16):
    gain = block_levels(own_key, dims, cuts, -0.22, 0.18) if cuts else 1.0
    values = jax.random.normal(own_key, dims, jnp.float32) * deviation * gain
    return jnp.minimum(jnp.maximum(values, -most), most).astype(held_as)


def setup_inputs(seed: int = 0, part: int = 0) -> dict:
    key_list = jax.random.split(jax.random.key(seed), 6)
    part_splits = jax.random.split(jax.random.fold_in(key_list[5], part), 6)
    return {
        "queries": draw_queries(jax.random.fold_in(jax.random.fold_in(key_list[5], part), 71), part),
        "keys": draw_keys(jax.random.fold_in(jax.random.fold_in(key_list[5], part), 71), part),
        "values": gaussian(part_splits[2], (2, TOKENS, E), 1.0, 6.0, ((0, 2), (1, 16))),
        "neighbours": draw_neighbours(jax.random.fold_in(jax.random.fold_in(key_list[5], part), 71), part),
        "w_out": gaussian(key_list[4], (E, D), E ** -0.5, 0.125),
    }


guidance_scale = 5.0


def tile_attention(q_tile, k_near, v_near):
    scores = jnp.einsum("qhd,khd->hqk", q_tile.astype(jnp.float32), k_near.astype(jnp.float32)) * (1.0 / HD ** 0.5)
    peak = jnp.max(scores, axis=-1, keepdims=True)
    expval = jnp.exp(scores - peak)
    weights = (expval / jnp.sum(expval, axis=-1, keepdims=True)).astype(jnp.bfloat16)
    result = jnp.einsum("hqk,khd->qhd", weights.astype(jnp.float32), v_near.astype(jnp.float32))
    return result.astype(jnp.bfloat16)


def reference(queries, keys, values, neighbours, w_out):
    def branch_output(branch_id):
        q_tiles = queries[branch_id].reshape(TILES, TILE, HEADS, HD)
        k_tiles = keys[branch_id].reshape(TILES, TILE, HEADS, HD)
        v_tiles = values[branch_id].reshape(TILES, TILE, HEADS, HD)

        def per_tile(tile_index):
            tile_ids = neighbours[tile_index]
            k_near = k_tiles[tile_ids].reshape(NB * TILE, HEADS, HD)
            v_near = v_tiles[tile_ids].reshape(NB * TILE, HEADS, HD)
            return tile_attention(q_tiles[tile_index], k_near, v_near)

        attended = lax.map(per_tile, jnp.arange(TILES, dtype=jnp.int32)).reshape(TOKENS, E)
        return jnp.dot(attended, w_out, preferred_element_type=jnp.float32)

    conditional = branch_output(0)
    unconditional = branch_output(1)
    return (unconditional + guidance_scale * (conditional - unconditional)).astype(jnp.bfloat16)
```

```python
import jax
import jax.numpy as jnp
import numpy as np
from jax import lax
from jax.experimental import pallas as pl
from jax.experimental.pallas import tpu as pltpu
from jax.sharding import PartitionSpec as P

HEADS = 16
HD = 128
TILE = 64
GUIDANCE = 5.0
MESH = pl.DeviceIdType.MESH

SEQ = 16
RING = 4
NB = 11
ROWS = 768
ROUNDS = 6
TILES = ROWS // TILE
PAIR = 2 * TILE
PAIRS = ROUNDS * SEQ
SPAN = NB * TILE
EXP_SCALE = float(np.log2(np.e) / HD**0.5)

OFFSETS = (
    (0, 1), (0, 3), (1, 0), (3, 0),
    (1, 1), (3, 3), (1, 3), (3, 1),
    (0, 2), (2, 0),
    (1, 2), (3, 2), (2, 1), (2, 3),
    (2, 2),
)


def kernel(
    ids, q_hbm, k_hbm, v_hbm, w_hbm, out_hbm,
    q_buf, k_buf, v_buf, w_buf, att, swapped, folded, gathered, out_buf,
    s_even, s_odd, p_even, p_odd,
    w_sem, out_sem, k_send, k_recv, v_send, v_recv, q_send, q_recv,
    x_send, x_recv, g_send, g_recv, f_send, f_recv,
):
    core = lax.axis_index("cfg")
    me = lax.axis_index("seq")
    z, y = me // RING, me % RING
    other_core = {"cfg": 1 - core}
    peers = [lax.rem(z + dz, RING) * RING + lax.rem(y + dy, RING) for dz, dy in OFFSETS]

    def await_bytes(ref, sem):
        pltpu.make_async_copy(ref, ref, sem).wait()

    barrier = pltpu.get_barrier_semaphore()
    for peer in peers:
        pl.semaphore_signal(barrier, inc=1, device_id={"seq": peer}, device_id_type=MESH)
    pl.semaphore_signal(barrier, inc=1, device_id=other_core, device_id_type=MESH)
    pl.semaphore_wait(barrier, SEQ)

    def head_cols(head):
        return pl.ds(pl.multiple_of(head * HD, HD), HD)

    def scatter(src, buf, send, recv):
        tiles = pl.ds(me * TILES, TILES)
        for peer in peers:
            pltpu.make_async_remote_copy(
                src_ref=src.at[0, :, :, head_cols(peer)],
                dst_ref=buf.at[tiles],
                send_sem=send,
                recv_sem=recv,
                device_id={"seq": peer},
                device_id_type=MESH,
            ).start()
        pltpu.make_async_copy(src.at[0, :, :, head_cols(me)], buf.at[tiles], recv).start()

    def scatter_queries(r, _):
        rows = pl.ds(pl.multiple_of(r * PAIR, PAIR), PAIR)
        for peer in peers:
            pltpu.make_async_remote_copy(
                src_ref=q_hbm.at[0, rows, head_cols(peer)],
                dst_ref=q_buf.at[r, me],
                send_sem=q_send,
                recv_sem=q_recv.at[r],
                device_id={"seq": peer},
                device_id_type=MESH,
            ).start()
        pltpu.make_async_copy(
            q_hbm.at[0, rows, head_cols(me)], q_buf.at[r, me], q_recv.at[r]
        ).start()
        return 0

    remote_tiles = pl.ds(0, (SEQ - 1) * TILES)
    scatter(k_hbm, k_buf, k_send, k_recv)
    half_cols = w_hbm.shape[1] // 2
    w_copy = pltpu.make_async_copy(
        w_hbm.at[:, pl.ds(pl.multiple_of(core * half_cols, half_cols), half_cols)], w_buf, w_sem
    )
    w_copy.start()
    for ref in (s_even, s_odd, p_even, p_odd):
        ref[...] = jnp.zeros_like(ref)
    await_bytes(k_buf.at[remote_tiles], k_send)
    scatter(v_hbm, v_buf, v_send, v_recv)
    await_bytes(v_buf.at[remote_tiles], v_send)
    lax.fori_loop(0, ROUNDS, scatter_queries, 0)
    await_bytes(k_buf, k_recv)
    await_bytes(v_buf, v_recv)
    w_copy.wait()

    def near(buf, tile):
        return jnp.concatenate([buf[ids[tile, j]] for j in range(NB)], axis=0)

    def near_pair(buf, pair):
        tile = (pair % SEQ) * TILES + (pair // SEQ) * 2
        return jnp.concatenate([near(buf, tile), near(buf, tile + 1)], axis=1)

    def step(i, scores_in, scores_out, probs_in, probs_out):
        done = jnp.maximum(i - 2, 0)
        result = lax.dot_general(
            probs_in[...], near_pair(v_buf, done), (((0,), (0,)), ((), ())),
            preferred_element_type=jnp.float32,
        )
        att[done // SEQ, 0, done % SEQ] = result[:TILE, :HD].astype(jnp.bfloat16)
        att[done // SEQ, 1, done % SEQ] = result[TILE:, HD:].astype(jnp.bfloat16)
        scores = scores_in[...]
        peak = jnp.max(scores, axis=0, keepdims=True) * EXP_SCALE
        expval = jnp.exp2(scores * EXP_SCALE - peak)
        total = jnp.sum(expval, axis=0, keepdims=True)
        probs_out[...] = (expval * (1.0 / total)).astype(jnp.bfloat16)
        pair = jnp.minimum(i, PAIRS - 1)
        queries = q_buf[pair // SEQ, pair % SEQ]
        zero = jnp.zeros((TILE, HD), jnp.bfloat16)
        blocks = jnp.concatenate(
            [
                jnp.concatenate([queries[:TILE], zero], axis=1),
                jnp.concatenate([zero, queries[TILE:]], axis=1),
            ],
            axis=0,
        )
        scores_out[...] = lax.dot_general(
            near_pair(k_buf, pair), blocks, (((1,), (1,)), ((), ())),
            preferred_element_type=jnp.float32,
        )

    def steps(first, count):
        def two(n, _):
            i = first + 2 * n
            step(i, s_odd, s_even, p_even, p_odd)
            step(i + 1, s_even, s_odd, p_odd, p_even)
            return 0

        lax.fori_loop(0, count // 2, two, 0)

    def swap(r):
        return pltpu.make_async_remote_copy(
            src_ref=att.at[r, 1 - core],
            dst_ref=swapped.at[r],
            send_sem=x_send,
            recv_sem=x_recv.at[r],
            device_id=other_core,
            device_id_type=MESH,
        )

    own_gain = jnp.where(core == 0, GUIDANCE, 1.0 - GUIDANCE).astype(jnp.float32)
    other_gain = 1.0 - own_gain

    def round_rows(r, half):
        return pl.ds(pl.multiple_of(r * PAIR + half * TILE, TILE), TILE)

    def fold(r):
        await_bytes(swapped.at[r], x_recv.at[r])

        def some(n, _):
            part = pl.ds(n * 4, 4)
            own = att[r, core, part].astype(jnp.float32)
            other = swapped[r, part].astype(jnp.float32)
            folded[r, part] = (own * own_gain + other * other_gain).astype(jnp.bfloat16)
            return 0

        lax.fori_loop(0, SEQ // 4, some, 0)
        rows = round_rows(r, core)
        for peer in peers:
            pltpu.make_async_remote_copy(
                src_ref=folded.at[r, peer],
                dst_ref=gathered.at[rows, head_cols(me)],
                send_sem=g_send,
                recv_sem=g_recv.at[r],
                device_id={"seq": peer},
                device_id_type=MESH,
            ).start()
        pltpu.make_async_copy(
            folded.at[r, me], gathered.at[rows, head_cols(me)], g_recv.at[r]
        ).start()

    def forward(r):
        rows = round_rows(r, core)
        await_bytes(gathered.at[rows], g_recv.at[r])
        pltpu.make_async_remote_copy(
            src_ref=gathered.at[rows],
            dst_ref=gathered.at[rows],
            send_sem=f_send,
            recv_sem=f_recv.at[r],
            device_id=other_core,
            device_id_type=MESH,
        ).start()

    def project(r):
        await_bytes(gathered.at[round_rows(r, 1 - core)], f_recv.at[r])
        rows = pl.ds(pl.multiple_of(r * PAIR, PAIR), PAIR)

        def columns(n, _):
            cols = pl.ds(pl.multiple_of(n * 512, 512), 512)
            out_buf[rows, cols] = jnp.dot(
                gathered[rows, :], w_buf[:, cols], preferred_element_type=jnp.float32
            ).astype(jnp.bfloat16)
            return 0

        lax.fori_loop(0, half_cols // 512, columns, 0)
        pltpu.make_async_copy(out_buf.at[rows], out_hbm.at[rows], out_sem).start()

    def one_round(r, _):
        await_bytes(q_buf.at[r], q_recv.at[r])
        steps(r * SEQ, 2)
        pl.when(r >= 1)(lambda: swap(r - 1).start())
        steps(r * SEQ + 2, 8)
        pl.when(r >= 1)(lambda: fold(r - 1))
        steps(r * SEQ + 10, 6)
        pl.when(r >= 1)(lambda: forward(r - 1))
        pl.when(r >= 2)(lambda: project(r - 2))
        return 0

    lax.fori_loop(0, ROUNDS, one_round, 0)
    steps(PAIRS, 2)
    last = ROUNDS - 1
    swap(last).start()
    project(last - 1)
    fold(last)
    forward(last)
    project(last)

    await_bytes(q_buf.at[:, pl.ds(0, SEQ - 1)], q_send)
    await_bytes(swapped, x_send)
    await_bytes(folded.at[:, pl.ds(0, SEQ - 1)], g_send)
    await_bytes(swapped, f_send)
    await_bytes(out_buf, out_sem)


def by_tile(tokens):
    return tokens.reshape(1, TILES, TILE, HEADS * HD)


def on_device(queries, keys, values, neighbours, w_out):
    bf16, f32 = jnp.bfloat16, jnp.float32
    dma = pltpu.SemaphoreType.DMA
    vmem = pltpu.VMEM
    width = w_out.shape[1] // 2
    return pl.pallas_call(
        kernel,
        out_shape=jax.ShapeDtypeStruct((ROWS, width), bf16),
        in_specs=[pl.BlockSpec(memory_space=pltpu.SMEM)]
        + [pl.BlockSpec(memory_space=pl.ANY)] * 4,
        out_specs=pl.BlockSpec(memory_space=pl.ANY),
        scratch_shapes=[
            vmem((ROUNDS, SEQ, PAIR, HD), bf16),
            vmem((SEQ * TILES, TILE, HD), bf16),
            vmem((SEQ * TILES, TILE, HD), bf16),
            vmem((HEADS * HD, width), bf16),
            vmem((ROUNDS, 2, SEQ, TILE, HD), bf16),
            vmem((ROUNDS, SEQ, TILE, HD), bf16),
            vmem((ROUNDS, SEQ, TILE, HD), bf16),
            vmem((ROWS, HEADS * HD), bf16),
            vmem((ROWS, width), bf16),
            vmem((SPAN, PAIR), f32),
            vmem((SPAN, PAIR), f32),
            vmem((SPAN, PAIR), bf16),
            vmem((SPAN, PAIR), bf16),
            dma, dma,
            dma, dma, dma, dma,
            dma, dma((ROUNDS,)),
            dma, dma((ROUNDS,)),
            dma, dma((ROUNDS,)),
            dma, dma((ROUNDS,)),
        ],
        compiler_params=pltpu.CompilerParams(
            collective_id=0, has_side_effects=True, vmem_limit_bytes=56 * 2**20
        ),
        cost_estimate=pl.CostEstimate(
            flops=11_000_000_000, bytes_accessed=20 * 2**20, transcendentals=8_700_000
        ),
    )(neighbours, queries, by_tile(keys), by_tile(values), w_out)


def solution(mesh):
    return jax.shard_map(
        on_device,
        mesh=mesh,
        in_specs=(
            P("cfg", ("batch", "seq"), None),
            P("cfg", ("batch", "seq"), None),
            P("cfg", ("batch", "seq"), None),
            P("batch", None),
            P(),
        ),
        out_specs=P(("batch", "seq"), "cfg"),
        check_vma=False,
    )
```

```python
import jax
import jax.numpy as jnp
import numpy as np
from jax import lax
from jax.experimental import pallas as pl
from jax.experimental.pallas import tpu as pltpu
from jax.sharding import PartitionSpec as P

HEADS = 16
HD = 128
TILE = 64
GUIDANCE = 5.0
MESH = pl.DeviceIdType.MESH

SEQ = 16
RING = 4
NB = 11
ROWS = 768
ROUNDS = 6
TILES = ROWS // TILE
BLK = 2
PAIR = 2 * TILE
PAIRS = ROUNDS * SEQ
SPAN = NB * TILE
EXP_SCALE = float(np.log2(np.e) / HD**0.5)

OFFSETS = (
    (0, 1), (0, 3), (1, 0), (3, 0),
    (1, 1), (3, 3), (1, 3), (3, 1),
    (0, 2), (2, 0),
    (1, 2), (3, 2), (2, 1), (2, 3),
    (2, 2),
)


def kernel(
    ids_hbm, q_hbm, k_hbm, v_hbm, w_hbm, out_hbm,
    q_buf, k_buf, v_buf, w_buf, att, swapped, folded, gathered,
    s_even, s_odd, p_even, p_odd,
    ids, ids_sem, w_sem, k_send, k_recv, v_send, v_recv, q_send, q_recv,
    x_send, x_recv, g_send, g_recv, f_send, f_recv,
):
    core = lax.axis_index("cfg")
    me = lax.axis_index("seq")
    z, y = me // RING, me % RING
    other_core = {"cfg": 1 - core}
    peers = [lax.rem(z + dz, RING) * RING + lax.rem(y + dy, RING) for dz, dy in OFFSETS]

    def await_bytes(ref, sem):
        pltpu.make_async_copy(ref, ref, sem).wait()

    barrier = pltpu.get_barrier_semaphore()
    for peer in peers:
        pl.semaphore_signal(barrier, inc=1, device_id={"seq": peer}, device_id_type=MESH)
    pl.semaphore_signal(barrier, inc=1, device_id=other_core, device_id_type=MESH)
    pl.semaphore_wait(barrier, SEQ)

    def head_cols(head):
        return pl.ds(pl.multiple_of(head * HD, HD), HD)

    def scatter(src, buf, send, recv):
        tiles = pl.ds(me * TILES, TILES)

        def block(n, _):
            for peer in peers:
                pltpu.make_async_remote_copy(
                    src_ref=src.at[0, pl.ds(n * BLK, BLK), :, head_cols(peer)],
                    dst_ref=buf.at[pl.ds(me * TILES + n * BLK, BLK)],
                    send_sem=send,
                    recv_sem=recv,
                    device_id={"seq": peer},
                    device_id_type=MESH,
                ).start()
            return 0

        lax.fori_loop(0, TILES // BLK, block, 0)
        pltpu.make_async_copy(src.at[0, :, :, head_cols(me)], buf.at[tiles], recv).start()

    def scatter_queries(r, _):
        rows = pl.ds(pl.multiple_of(r * PAIR, PAIR), PAIR)
        for peer in peers:
            pltpu.make_async_remote_copy(
                src_ref=q_hbm.at[0, rows, head_cols(peer)],
                dst_ref=q_buf.at[r, me],
                send_sem=q_send,
                recv_sem=q_recv.at[r],
                device_id={"seq": peer},
                device_id_type=MESH,
            ).start()
        pltpu.make_async_copy(
            q_hbm.at[0, rows, head_cols(me)], q_buf.at[r, me], q_recv.at[r]
        ).start()
        return 0

    remote_tiles = pl.ds(0, (SEQ - 1) * TILES)
    scatter(k_hbm, k_buf, k_send, k_recv)
    half_cols = w_hbm.shape[1] // 2
    w_copy = pltpu.make_async_copy(
        w_hbm.at[:, pl.ds(pl.multiple_of(core * half_cols, half_cols), half_cols)], w_buf, w_sem
    )
    w_copy.start()
    ids_copy = pltpu.make_async_copy(ids_hbm, ids, ids_sem)
    ids_copy.start()
    for ref in (s_even, s_odd, p_even, p_odd):
        ref[...] = jnp.zeros_like(ref)
    scatter(v_hbm, v_buf, v_send, v_recv)
    lax.fori_loop(0, ROUNDS, scatter_queries, 0)
    await_bytes(k_buf.at[remote_tiles], k_send)
    await_bytes(v_buf.at[remote_tiles], v_send)
    await_bytes(k_buf, k_recv)
    await_bytes(v_buf, v_recv)
    w_copy.wait()
    ids_copy.wait()

    def near(buf, tile):
        return jnp.concatenate([buf[ids[tile, j]] for j in range(NB)], axis=0)

    def near_pair(buf, pair):
        tile = (pair % SEQ) * TILES + (pair // SEQ) * 2
        return jnp.concatenate([near(buf, tile), near(buf, tile + 1)], axis=1)

    def step(i, scores_in, scores_out, probs_in, probs_out):
        done = jnp.maximum(i - 2, 0)
        result = lax.dot_general(
            probs_in[...], near_pair(v_buf, done), (((0,), (0,)), ((), ())),
            preferred_element_type=jnp.float32,
        )
        att[done // SEQ, 0, done % SEQ] = result[:TILE, :HD].astype(jnp.bfloat16)
        att[done // SEQ, 1, done % SEQ] = result[TILE:, HD:].astype(jnp.bfloat16)
        scores = scores_in[...]
        peak = jnp.max(scores, axis=0, keepdims=True) * EXP_SCALE
        expval = jnp.exp2(scores * EXP_SCALE - peak)
        total = jnp.sum(expval, axis=0, keepdims=True)
        probs_out[...] = (expval * (1.0 / total)).astype(jnp.bfloat16)
        pair = jnp.minimum(i, PAIRS - 1)
        queries = q_buf[pair // SEQ, pair % SEQ]
        zero = jnp.zeros((TILE, HD), jnp.bfloat16)
        blocks = jnp.concatenate(
            [
                jnp.concatenate([queries[:TILE], zero], axis=1),
                jnp.concatenate([zero, queries[TILE:]], axis=1),
            ],
            axis=0,
        )
        scores_out[...] = lax.dot_general(
            near_pair(k_buf, pair), blocks, (((1,), (1,)), ((), ())),
            preferred_element_type=jnp.float32,
        )

    def steps(first, count):
        def two(n, _):
            i = first + 2 * n
            step(i, s_odd, s_even, p_even, p_odd)
            step(i + 1, s_even, s_odd, p_odd, p_even)
            return 0

        lax.fori_loop(0, count // 2, two, 0)

    def swap(r):
        return pltpu.make_async_remote_copy(
            src_ref=att.at[r, 1 - core],
            dst_ref=swapped.at[r],
            send_sem=x_send,
            recv_sem=x_recv.at[r],
            device_id=other_core,
            device_id_type=MESH,
        )

    own_gain = jnp.where(core == 0, GUIDANCE, 1.0 - GUIDANCE).astype(jnp.float32)
    other_gain = 1.0 - own_gain

    def round_rows(r, half):
        return pl.ds(pl.multiple_of(r * PAIR + half * TILE, TILE), TILE)

    def fold(r):
        await_bytes(swapped.at[r], x_recv.at[r])

        def some(n, _):
            part = pl.ds(n * 4, 4)
            own = att[r, core, part].astype(jnp.float32)
            other = swapped[r, part].astype(jnp.float32)
            folded[r, part] = (own * own_gain + other * other_gain).astype(jnp.bfloat16)
            return 0

        lax.fori_loop(0, SEQ // 4, some, 0)
        rows = round_rows(r, core)
        for peer in peers:
            pltpu.make_async_remote_copy(
                src_ref=folded.at[r, peer],
                dst_ref=gathered.at[rows, head_cols(me)],
                send_sem=g_send,
                recv_sem=g_recv.at[r],
                device_id={"seq": peer},
                device_id_type=MESH,
            ).start()
        pltpu.make_async_copy(
            folded.at[r, me], gathered.at[rows, head_cols(me)], g_recv.at[r]
        ).start()

    def forward(r):
        rows = round_rows(r, core)
        await_bytes(gathered.at[rows], g_recv.at[r])
        pltpu.make_async_remote_copy(
            src_ref=gathered.at[rows],
            dst_ref=gathered.at[rows],
            send_sem=f_send,
            recv_sem=f_recv.at[r],
            device_id=other_core,
            device_id_type=MESH,
        ).start()

    def project(r):
        await_bytes(gathered.at[round_rows(r, 1 - core)], f_recv.at[r])
        rows = pl.ds(pl.multiple_of(r * PAIR, PAIR), PAIR)

        def columns(n, _):
            cols = pl.ds(pl.multiple_of(n * 512, 512), 512)
            out_hbm[rows, cols] = jnp.dot(
                gathered[rows, :], w_buf[:, cols], preferred_element_type=jnp.float32
            ).astype(jnp.bfloat16)
            return 0

        lax.fori_loop(0, half_cols // 512, columns, 0)

    def one_round(r, _):
        await_bytes(q_buf.at[r], q_recv.at[r])
        steps(r * SEQ, 2)
        pl.when(r >= 1)(lambda: swap(r - 1).start())
        steps(r * SEQ + 2, 8)
        pl.when(r >= 1)(lambda: fold(r - 1))
        steps(r * SEQ + 10, 6)
        return 0

    lax.fori_loop(0, ROUNDS, one_round, 0)
    steps(PAIRS, 2)
    last = ROUNDS - 1
    swap(last).start()
    fold(last)
    forward(0)

    def finish(r, _):
        forward(r + 1)
        project(r)
        return 0

    lax.fori_loop(0, last, finish, 0)
    project(last)

    await_bytes(q_buf.at[:, pl.ds(0, SEQ - 1)], q_send)
    await_bytes(swapped, x_send)
    await_bytes(folded.at[:, pl.ds(0, SEQ - 1)], g_send)
    await_bytes(swapped, f_send)


def by_tile(tokens):
    return tokens.reshape(1, TILES, TILE, HEADS * HD)


def on_device(queries, keys, values, neighbours, w_out):
    bf16, f32 = jnp.bfloat16, jnp.float32
    dma = pltpu.SemaphoreType.DMA
    vmem = pltpu.VMEM
    width = w_out.shape[1] // 2
    return pl.pallas_call(
        kernel,
        out_shape=pltpu.VMEM((ROWS, width), bf16),
        in_specs=[pl.BlockSpec(memory_space=pl.ANY)] * 5,
        out_specs=pl.BlockSpec(memory_space=pltpu.VMEM),
        scratch_shapes=[
            vmem((ROUNDS, SEQ, PAIR, HD), bf16),
            vmem((SEQ * TILES, TILE, HD), bf16),
            vmem((SEQ * TILES, TILE, HD), bf16),
            vmem((HEADS * HD, width), bf16),
            vmem((ROUNDS, 2, SEQ, TILE, HD), bf16),
            vmem((ROUNDS, SEQ, TILE, HD), bf16),
            vmem((ROUNDS, SEQ, TILE, HD), bf16),
            vmem((ROWS, HEADS * HD), bf16),
            vmem((SPAN, PAIR), f32),
            vmem((SPAN, PAIR), f32),
            vmem((SPAN, PAIR), bf16),
            vmem((SPAN, PAIR), bf16),
            pltpu.SMEM((SEQ * TILES, NB), jnp.int32), dma, dma,
            dma, dma, dma, dma,
            dma, dma((ROUNDS,)),
            dma, dma((ROUNDS,)),
            dma, dma((ROUNDS,)),
            dma, dma((ROUNDS,)),
        ],
        compiler_params=pltpu.CompilerParams(
            collective_id=0, has_side_effects=True, vmem_limit_bytes=56 * 2**20
        ),
        cost_estimate=pl.CostEstimate(
            flops=11_000_000_000, bytes_accessed=20 * 2**20, transcendentals=8_700_000
        ),
    )(neighbours, queries, by_tile(keys), by_tile(values), w_out)


def solution(mesh):
    return jax.shard_map(
        on_device,
        mesh=mesh,
        in_specs=(
            P("cfg", ("batch", "seq"), None),
            P("cfg", ("batch", "seq"), None),
            P("cfg", ("batch", "seq"), None),
            P("batch", None),
            P(),
        ),
        out_specs=P(("batch", "seq"), "cfg"),
        check_vma=False,
    )
```

```python
import jax
import jax.numpy as jnp
import numpy as np
from jax import lax
from jax.experimental import pallas as pl
from jax.experimental.pallas import tpu as pltpu
from jax.sharding import PartitionSpec as P

HEADS = 16
HD = 128
TILE = 64
GUIDANCE = 5.0
MESH = pl.DeviceIdType.MESH

SEQ = 16
RING = 4
NB = 11
ROWS = 768
ROUNDS = 6
TILES = ROWS // TILE
BLK = 2
STORES = 4
PAIR = 2 * TILE
PAIRS = ROUNDS * SEQ
SPAN = NB * TILE
EXP_SCALE = float(np.log2(np.e) / HD**0.5)

OFFSETS = (
    (0, 1), (0, 3), (1, 0), (3, 0),
    (1, 1), (3, 3), (1, 3), (3, 1),
    (0, 2), (2, 0),
    (1, 2), (3, 2), (2, 1), (2, 3),
    (2, 2),
)


def kernel(
    ids_hbm, q_hbm, k_hbm, v_hbm, w_hbm, out_ref, last_ref, w_buf,
    q_buf, k_buf, v_buf, att, swapped, folded, gathered,
    s_even, s_odd, p_even, p_odd,
    ids, ids_sem, w_sem, k_send, k_recv, v_send, v_recv, q_send, q_recv,
    x_send, x_recv, g_send, g_recv, f_send, f_recv,
):
    core = lax.axis_index("cfg")
    me = lax.axis_index("seq")
    z, y = me // RING, me % RING
    other_core = {"cfg": 1 - core}
    peers = [lax.rem(z + dz, RING) * RING + lax.rem(y + dy, RING) for dz, dy in OFFSETS]

    def await_bytes(ref, sem):
        pltpu.make_async_copy(ref, ref, sem).wait()

    barrier = pltpu.get_barrier_semaphore()
    for peer in peers:
        pl.semaphore_signal(barrier, inc=1, device_id={"seq": peer}, device_id_type=MESH)
    pl.semaphore_signal(barrier, inc=1, device_id=other_core, device_id_type=MESH)
    pl.semaphore_wait(barrier, SEQ)

    def head_cols(head):
        return pl.ds(pl.multiple_of(head * HD, HD), HD)

    def scatter(src, buf, send, recv):
        tiles = pl.ds(me * TILES, TILES)

        def block(n, _):
            for peer in peers:
                pltpu.make_async_remote_copy(
                    src_ref=src.at[0, pl.ds(n * BLK, BLK), :, head_cols(peer)],
                    dst_ref=buf.at[pl.ds(me * TILES + n * BLK, BLK)],
                    send_sem=send,
                    recv_sem=recv,
                    device_id={"seq": peer},
                    device_id_type=MESH,
                ).start()
            return 0

        lax.fori_loop(0, TILES // BLK, block, 0)
        pltpu.make_async_copy(src.at[0, :, :, head_cols(me)], buf.at[tiles], recv).start()

    def scatter_queries(r, _):
        rows = pl.ds(pl.multiple_of(r * PAIR, PAIR), PAIR)
        for peer in peers:
            pltpu.make_async_remote_copy(
                src_ref=q_hbm.at[0, rows, head_cols(peer)],
                dst_ref=q_buf.at[r, me],
                send_sem=q_send,
                recv_sem=q_recv.at[r],
                device_id={"seq": peer},
                device_id_type=MESH,
            ).start()
        pltpu.make_async_copy(
            q_hbm.at[0, rows, head_cols(me)], q_buf.at[r, me], q_recv.at[r]
        ).start()
        return 0

    remote_tiles = pl.ds(0, (SEQ - 1) * TILES)
    scatter(k_hbm, k_buf, k_send, k_recv)
    half_cols = w_hbm.shape[1] // 2
    w_copy = pltpu.make_async_copy(
        w_hbm.at[:, pl.ds(pl.multiple_of(core * half_cols, half_cols), half_cols)], w_buf, w_sem
    )
    w_copy.start()
    ids_copy = pltpu.make_async_copy(ids_hbm, ids, ids_sem)
    ids_copy.start()
    for ref in (s_even, s_odd, p_even, p_odd):
        ref[...] = jnp.zeros_like(ref)
    scatter(v_hbm, v_buf, v_send, v_recv)
    lax.fori_loop(0, ROUNDS, scatter_queries, 0)
    await_bytes(k_buf.at[remote_tiles], k_send)
    await_bytes(v_buf.at[remote_tiles], v_send)
    await_bytes(k_buf, k_recv)
    await_bytes(v_buf, v_recv)
    w_copy.wait()
    ids_copy.wait()

    def near(buf, tile):
        return jnp.concatenate([buf[ids[j, tile]] for j in range(NB)], axis=0)

    def near_pair(buf, pair):
        tile = (pair % SEQ) * TILES + (pair // SEQ) * 2
        return jnp.concatenate([near(buf, tile), near(buf, tile + 1)], axis=1)

    def step(i, scores_in, scores_out, probs_in, probs_out):
        done = jnp.maximum(i - 2, 0)
        result = lax.dot_general(
            probs_in[...], near_pair(v_buf, done), (((0,), (0,)), ((), ())),
            preferred_element_type=jnp.float32,
        )
        att[done // SEQ, 0, done % SEQ] = result[:TILE, :HD].astype(jnp.bfloat16)
        att[done // SEQ, 1, done % SEQ] = result[TILE:, HD:].astype(jnp.bfloat16)
        scores = scores_in[...]
        peak = jnp.max(scores, axis=0, keepdims=True) * EXP_SCALE
        expval = jnp.exp2(scores * EXP_SCALE - peak)
        total = jnp.sum(expval, axis=0, keepdims=True)
        probs_out[...] = (expval * (1.0 / total)).astype(jnp.bfloat16)
        pair = jnp.minimum(i, PAIRS - 1)
        queries = q_buf[pair // SEQ, pair % SEQ]
        zero = jnp.zeros((TILE, HD), jnp.bfloat16)
        blocks = jnp.concatenate(
            [
                jnp.concatenate([queries[:TILE], zero], axis=1),
                jnp.concatenate([zero, queries[TILE:]], axis=1),
            ],
            axis=0,
        )
        scores_out[...] = lax.dot_general(
            near_pair(k_buf, pair), blocks, (((1,), (1,)), ((), ())),
            preferred_element_type=jnp.float32,
        )

    def steps(first, count):
        def two(n, _):
            i = first + 2 * n
            step(i, s_odd, s_even, p_even, p_odd)
            step(i + 1, s_even, s_odd, p_odd, p_even)
            return 0

        lax.fori_loop(0, count // 2, two, 0)

    def swap(r):
        return pltpu.make_async_remote_copy(
            src_ref=att.at[r, 1 - core],
            dst_ref=swapped.at[r],
            send_sem=x_send,
            recv_sem=x_recv.at[r],
            device_id=other_core,
            device_id_type=MESH,
        )

    own_gain = jnp.where(core == 0, GUIDANCE, 1.0 - GUIDANCE).astype(jnp.float32)
    other_gain = 1.0 - own_gain

    def round_rows(r, half):
        return pl.ds(pl.multiple_of(r * PAIR + half * TILE, TILE), TILE)

    def fold(r):
        await_bytes(swapped.at[r], x_recv.at[r])

        def some(n, _):
            part = pl.ds(n * 4, 4)
            own = att[r, core, part].astype(jnp.float32)
            other = swapped[r, part].astype(jnp.float32)
            folded[r, part] = (own * own_gain + other * other_gain).astype(jnp.bfloat16)
            return 0

        lax.fori_loop(0, SEQ // 4, some, 0)
        rows = round_rows(r, core)
        for peer in peers:
            pltpu.make_async_remote_copy(
                src_ref=folded.at[r, peer],
                dst_ref=gathered.at[rows, head_cols(me)],
                send_sem=g_send,
                recv_sem=g_recv.at[r],
                device_id={"seq": peer},
                device_id_type=MESH,
            ).start()
        pltpu.make_async_copy(
            folded.at[r, me], gathered.at[rows, head_cols(me)], g_recv.at[r]
        ).start()

    def forward(r):
        rows = round_rows(r, core)
        await_bytes(gathered.at[rows], g_recv.at[r])
        pltpu.make_async_remote_copy(
            src_ref=gathered.at[rows],
            dst_ref=gathered.at[rows],
            send_sem=f_send,
            recv_sem=f_recv.at[r],
            device_id=other_core,
            device_id_type=MESH,
        ).start()

    def project(r):
        await_bytes(gathered.at[round_rows(r, 1 - core)], f_recv.at[r])
        rows = pl.ds(pl.multiple_of(r * PAIR, PAIR), PAIR)

        def columns(n, _):
            cols = pl.ds(pl.multiple_of(n * 512, 512), 512)
            out_ref[rows, cols] = jnp.dot(
                gathered[rows, :], w_buf[:, cols], preferred_element_type=jnp.float32
            ).astype(jnp.bfloat16)
            return 0

        lax.fori_loop(0, half_cols // 512, columns, 0)

    def one_round(r, _):
        await_bytes(q_buf.at[r], q_recv.at[r])
        steps(r * SEQ, 2)
        pl.when(r >= 1)(lambda: swap(r - 1).start())
        steps(r * SEQ + 2, 8)
        pl.when(r >= 1)(lambda: fold(r - 1))
        steps(r * SEQ + 10, 6)
        return 0

    lax.fori_loop(0, ROUNDS, one_round, 0)
    steps(PAIRS, 2)
    last = ROUNDS - 1
    swap(last).start()
    fold(last)
    forward(0)

    def finish(r, _):
        forward(r + 1)
        project(r)
        return 0

    lax.fori_loop(0, last, finish, 0)
    await_bytes(gathered.at[round_rows(last, 1 - core)], f_recv.at[last])
    last_ref[...] = gathered[pl.ds(last * PAIR, PAIR), :]

    await_bytes(q_buf.at[:, pl.ds(0, SEQ - 1)], q_send)
    await_bytes(swapped, x_send)
    await_bytes(folded.at[:, pl.ds(0, SEQ - 1)], g_send)
    await_bytes(swapped, f_send)


def finish_kernel(done, last_rows, w_half, out_hbm, last_out, sems, last_sem):
    size = done.shape[0] // STORES
    stores = [
        pltpu.make_async_copy(
            done.at[pl.ds(n * size, size)], out_hbm.at[pl.ds(n * size, size)], sems.at[n]
        )
        for n in range(STORES)
    ]
    for store in stores:
        store.start()
    step = 512
    for n in range(last_out.shape[1] // step):
        cols = pl.ds(n * step, step)
        last_out[:, cols] = jnp.dot(
            last_rows[...], w_half[:, cols], preferred_element_type=jnp.float32
        ).astype(jnp.bfloat16)
    store = pltpu.make_async_copy(last_out, out_hbm.at[pl.ds(done.shape[0], PAIR)], last_sem)
    store.start()
    for each in (*stores, store):
        each.wait()


def by_tile(tokens):
    return tokens.reshape(1, TILES, TILE, HEADS * HD)


def on_device(queries, keys, values, neighbours, w_out):
    bf16, f32 = jnp.bfloat16, jnp.float32
    dma = pltpu.SemaphoreType.DMA
    vmem = pltpu.VMEM
    width = w_out.shape[1] // 2
    done, last_rows, w_half = pl.pallas_call(
        kernel,
        out_shape=(
            vmem((ROWS - PAIR, width), bf16),
            vmem((PAIR, HEADS * HD), bf16),
            vmem((HEADS * HD, width), bf16),
        ),
        in_specs=[pl.BlockSpec(memory_space=pl.ANY)] * 5,
        out_specs=[pl.BlockSpec(memory_space=vmem)] * 3,
        scratch_shapes=[
            vmem((ROUNDS, SEQ, PAIR, HD), bf16),
            vmem((SEQ * TILES, TILE, HD), bf16),
            vmem((SEQ * TILES, TILE, HD), bf16),
            vmem((ROUNDS, 2, SEQ, TILE, HD), bf16),
            vmem((ROUNDS, SEQ, TILE, HD), bf16),
            vmem((ROUNDS, SEQ, TILE, HD), bf16),
            vmem((ROWS, HEADS * HD), bf16),
            vmem((SPAN, PAIR), f32),
            vmem((SPAN, PAIR), f32),
            vmem((SPAN, PAIR), bf16),
            vmem((SPAN, PAIR), bf16),
            pltpu.SMEM((NB, SEQ * TILES), jnp.int32), dma, dma,
            dma, dma, dma, dma,
            dma, dma((ROUNDS,)),
            dma, dma((ROUNDS,)),
            dma, dma((ROUNDS,)),
            dma, dma((ROUNDS,)),
        ],
        compiler_params=pltpu.CompilerParams(
            collective_id=0, has_side_effects=True, vmem_limit_bytes=50 * 2**20
        ),
        cost_estimate=pl.CostEstimate(
            flops=11_000_000_000, bytes_accessed=20 * 2**20, transcendentals=8_700_000
        ),
    )(neighbours.T, queries, by_tile(keys), by_tile(values), w_out)
    return pl.pallas_call(
        finish_kernel,
        out_shape=jax.ShapeDtypeStruct((ROWS, width), bf16),
        in_specs=[pl.BlockSpec(memory_space=vmem)] * 3,
        out_specs=pl.BlockSpec(memory_space=pl.ANY),
        scratch_shapes=[vmem((PAIR, width), bf16), dma((STORES,)), dma],
        compiler_params=pltpu.CompilerParams(vmem_limit_bytes=40 * 2**20),
    )(done, last_rows, w_half)


def solution(mesh):
    return jax.shard_map(
        on_device,
        mesh=mesh,
        in_specs=(
            P("cfg", ("batch", "seq"), None),
            P("cfg", ("batch", "seq"), None),
            P("cfg", ("batch", "seq"), None),
            P("batch", None),
            P(),
        ),
        out_specs=P(("batch", "seq"), "cfg"),
        check_vma=False,
    )
```

```python
import jax
import jax.numpy as jnp
import numpy as np
from jax import lax
from jax.experimental import pallas as pl
from jax.experimental.pallas import tpu as pltpu
from jax.sharding import PartitionSpec as P

HEADS = 16
HD = 128
TILE = 64
GUIDANCE = 5.0
MESH = pl.DeviceIdType.MESH

SEQ = 16
RING = 4
NB = 11
ROWS = 768
ROUNDS = 6
TILES = ROWS // TILE
MIXED = (
    (1, 2), (3, 0), (0, 1), (2, 3), (3, 2), (1, 0), (0, 3), (2, 1),
    (2, 2), (1, 1), (3, 3), (0, 2), (2, 0), (1, 3), (3, 1),
)
BLK = 2
NEAR = 9
STORES = 4
COLS = 512
PAIR = 2 * TILE
PAIRS = ROUNDS * SEQ
SPAN = NB * TILE
EXP_SCALE = float(np.log2(np.e) / HD**0.5)

OFFSETS = (
    (0, 1), (0, 3), (1, 0), (3, 0),
    (1, 1), (3, 3), (1, 3), (3, 1),
    (0, 2), (2, 0),
    (1, 2), (3, 2), (2, 1), (2, 3),
    (2, 2),
)


def kernel(
    ids_hbm, q_hbm, k_hbm, v_hbm, w_hbm, out_ref, last_ref, w_buf,
    q_buf, k_buf, v_buf, att, swapped, folded, gathered,
    s_even, s_odd, p_even, p_odd,
    ids, ids_sem, w_sem, k_send, k_recv, v_send, v_recv, q_send, q_recv,
    x_send, x_recv, g_send, g_recv, f_send, f_recv,
):
    core = lax.axis_index("cfg")
    me = lax.axis_index("seq")
    z, y = me // RING, me % RING
    other_core = {"cfg": 1 - core}
    peers = [lax.rem(z + dz, RING) * RING + lax.rem(y + dy, RING) for dz, dy in OFFSETS]

    def await_bytes(ref, sem):
        pltpu.make_async_copy(ref, ref, sem).wait()

    mixed = [lax.rem(z + dz, RING) * RING + lax.rem(y + dy, RING) for dz, dy in MIXED]

    barrier = pltpu.get_barrier_semaphore()
    for peer in peers:
        pl.semaphore_signal(barrier, inc=1, device_id={"seq": peer}, device_id_type=MESH)
    pl.semaphore_signal(barrier, inc=1, device_id=other_core, device_id_type=MESH)
    pl.semaphore_wait(barrier, SEQ)

    def head_cols(head):
        return pl.ds(pl.multiple_of(head * HD, HD), HD)

    def scatter(src, buf, send, recv):
        tiles = pl.ds(me * TILES, TILES)

        def block(n, _):
            for peer in mixed:
                pltpu.make_async_remote_copy(
                    src_ref=src.at[0, pl.ds(n * BLK, BLK), :, head_cols(peer)],
                    dst_ref=buf.at[pl.ds(me * TILES + n * BLK, BLK)],
                    send_sem=send,
                    recv_sem=recv,
                    device_id={"seq": peer},
                    device_id_type=MESH,
                ).start()
            return 0

        lax.fori_loop(0, TILES // BLK, block, 0)
        pltpu.make_async_copy(src.at[0, :, :, head_cols(me)], buf.at[tiles], recv).start()

    def scatter_queries(r, recv_of):
        rows = pl.ds(pl.multiple_of(r * PAIR, PAIR), PAIR)
        for n, peer in enumerate(peers):
            pltpu.make_async_remote_copy(
                src_ref=q_hbm.at[0, rows, head_cols(peer)],
                dst_ref=q_buf.at[r, me],
                send_sem=q_send,
                recv_sem=recv_of(n),
                device_id={"seq": peer},
                device_id_type=MESH,
            ).start()
        pltpu.make_async_copy(
            q_hbm.at[0, rows, head_cols(me)], q_buf.at[r, me], recv_of(0)
        ).start()

    def scatter_later_queries(r, _):
        scatter_queries(r, lambda _: q_recv.at[r + 1])
        return 0

    remote_tiles = pl.ds(0, (SEQ - 1) * TILES)
    scatter(k_hbm, k_buf, k_send, k_recv)
    half_cols = w_hbm.shape[1] // 2
    w_copy = pltpu.make_async_copy(
        w_hbm.at[:, pl.ds(pl.multiple_of(core * half_cols, half_cols), half_cols)], w_buf, w_sem
    )
    w_copy.start()
    ids_copy = pltpu.make_async_copy(ids_hbm, ids, ids_sem)
    ids_copy.start()
    for ref in (s_even, s_odd, p_even, p_odd):
        ref[...] = jnp.zeros_like(ref)
    scatter(v_hbm, v_buf, v_send, v_recv)
    scatter_queries(0, lambda n: q_recv.at[n // (NEAR - 1)])
    lax.fori_loop(1, ROUNDS, scatter_later_queries, 0)
    await_bytes(k_buf.at[remote_tiles], k_send)
    await_bytes(v_buf.at[remote_tiles], v_send)
    await_bytes(k_buf, k_recv)
    await_bytes(v_buf, v_recv)
    w_copy.wait()
    ids_copy.wait()

    def near(buf, tile):
        return jnp.concatenate([buf[ids[j, tile]] for j in range(NB)], axis=0)

    def source(pair):
        n = pair % SEQ
        far = n // NEAR
        k = n - NEAR
        side = jnp.maximum(k, 0) // RING
        dz = (1 - far) * (n // 3 - 1) + far * ((1 - side) * 2 + side * (k - RING - 1))
        dy = (1 - far) * (n % 3 - 1) + far * ((1 - side) * k + side * 2)
        return (z + dz + RING) % RING * RING + (y + dy + RING) % RING

    def near_pair(buf, pair):
        tile = source(pair) * TILES + (pair // SEQ) * 2
        return jnp.concatenate([near(buf, tile), near(buf, tile + 1)], axis=1)

    def step(i, scores_in, scores_out, probs_in, probs_out):
        done = jnp.maximum(i - 2, 0)
        result = lax.dot_general(
            probs_in[...], near_pair(v_buf, done), (((0,), (0,)), ((), ())),
            preferred_element_type=jnp.float32,
        )
        att[done // SEQ, 0, source(done)] = result[:TILE, :HD].astype(jnp.bfloat16)
        att[done // SEQ, 1, source(done)] = result[TILE:, HD:].astype(jnp.bfloat16)
        scores = scores_in[...]
        peak = jnp.max(scores, axis=0, keepdims=True) * EXP_SCALE
        expval = jnp.exp2(scores * EXP_SCALE - peak)
        total = jnp.sum(expval, axis=0, keepdims=True)
        probs_out[...] = (expval * (1.0 / total)).astype(jnp.bfloat16)
        pair = jnp.minimum(i, PAIRS - 1)
        queries = q_buf[pair // SEQ, source(pair)]
        zero = jnp.zeros((TILE, HD), jnp.bfloat16)
        blocks = jnp.concatenate(
            [
                jnp.concatenate([queries[:TILE], zero], axis=1),
                jnp.concatenate([zero, queries[TILE:]], axis=1),
            ],
            axis=0,
        )
        scores_out[...] = lax.dot_general(
            near_pair(k_buf, pair), blocks, (((1,), (1,)), ((), ())),
            preferred_element_type=jnp.float32,
        )

    def steps(first, count):
        def two(n, _):
            i = first + 2 * n
            step(i, s_odd, s_even, p_even, p_odd)
            step(i + 1, s_even, s_odd, p_odd, p_even)
            return 0

        lax.fori_loop(0, count // 2, two, 0)

    def swap(r):
        return pltpu.make_async_remote_copy(
            src_ref=att.at[r, 1 - core],
            dst_ref=swapped.at[r],
            send_sem=x_send,
            recv_sem=x_recv.at[r],
            device_id=other_core,
            device_id_type=MESH,
        )

    own_gain = jnp.where(core == 0, GUIDANCE, 1.0 - GUIDANCE).astype(jnp.float32)
    other_gain = 1.0 - own_gain

    def round_rows(r, half):
        return pl.ds(pl.multiple_of(r * PAIR + half * TILE, TILE), TILE)

    def fold(r):
        await_bytes(swapped.at[r], x_recv.at[r])

        def some(n, _):
            part = pl.ds(n * 4, 4)
            own = att[r, core, part].astype(jnp.float32)
            other = swapped[r, part].astype(jnp.float32)
            folded[r, part] = (own * own_gain + other * other_gain).astype(jnp.bfloat16)
            return 0

        lax.fori_loop(0, SEQ // 4, some, 0)
        rows = round_rows(r, core)
        for peer in peers:
            pltpu.make_async_remote_copy(
                src_ref=folded.at[r, peer],
                dst_ref=gathered.at[rows, head_cols(me)],
                send_sem=g_send,
                recv_sem=g_recv.at[r],
                device_id={"seq": peer},
                device_id_type=MESH,
            ).start()
        pltpu.make_async_copy(
            folded.at[r, me], gathered.at[rows, head_cols(me)], g_recv.at[r]
        ).start()

    def forward(r):
        rows = round_rows(r, core)
        await_bytes(gathered.at[rows], g_recv.at[r])
        pltpu.make_async_remote_copy(
            src_ref=gathered.at[rows],
            dst_ref=gathered.at[rows],
            send_sem=f_send,
            recv_sem=f_recv.at[r],
            device_id=other_core,
            device_id_type=MESH,
        ).start()

    def project(r, rounds, first, count):
        rows = pl.ds(pl.multiple_of(r * PAIR, PAIR), rounds * PAIR)

        def columns(n, _):
            cols = pl.ds(pl.multiple_of(n * COLS, COLS), COLS)
            out_ref[rows, cols] = jnp.dot(
                gathered[rows, :], w_buf[:, cols], preferred_element_type=jnp.float32
            ).astype(jnp.bfloat16)
            return 0

        lax.fori_loop(first, first + count, columns, 0)

    def await_forward(r):
        await_bytes(gathered.at[round_rows(r, 1 - core)], f_recv.at[r])

    def one_round(r, _):
        await_bytes(q_buf.at[r], q_recv.at[r + 1])
        steps(r * SEQ, 2)
        swap(r - 1).start()
        steps(r * SEQ + 2, 8)
        fold(r - 1)
        steps(r * SEQ + 10, 6)
        return 0

    await_bytes(q_buf.at[0, pl.ds(0, NEAR)], q_recv.at[0])
    steps(0, NEAR - 1)
    await_bytes(q_buf.at[0, pl.ds(0, SEQ - NEAR)], q_recv.at[1])
    steps(NEAR - 1, SEQ - NEAR + 1)
    lax.fori_loop(1, ROUNDS, one_round, 0)
    steps(PAIRS, 2)
    last = ROUNDS - 1
    swap(last).start()
    fold(last)
    blocks = half_cols // COLS
    forward(0)
    forward(1)
    forward(2)
    await_forward(0)
    await_forward(1)
    project(0, 2, 0, 4)
    forward(3)
    await_forward(2)
    project(2, 1, 0, 4)
    forward(4)
    await_forward(3)
    project(3, 1, 0, 4)
    forward(5)
    await_forward(4)
    project(4, 1, 0, 4)
    await_forward(5)
    last_ref[...] = gathered[pl.ds(last * PAIR, PAIR), :]

    await_bytes(q_buf.at[:, pl.ds(0, SEQ - 1)], q_send)
    await_bytes(swapped, x_send)
    await_bytes(folded.at[:, pl.ds(0, SEQ - 1)], g_send)
    await_bytes(swapped, f_send)


def finish_kernel(done, last_rows, w_half, out_hbm, last_out, sems, last_sem):
    size = done.shape[0] // STORES
    stores = [
        pltpu.make_async_copy(
            done.at[pl.ds(n * size, size)], out_hbm.at[pl.ds(n * size, size)], sems.at[n]
        )
        for n in range(STORES)
    ]
    for store in stores:
        store.start()
    step = 512
    for n in range(last_out.shape[1] // step):
        cols = pl.ds(n * step, step)
        last_out[:, cols] = jnp.dot(
            last_rows[...], w_half[:, cols], preferred_element_type=jnp.float32
        ).astype(jnp.bfloat16)
    store = pltpu.make_async_copy(last_out, out_hbm.at[pl.ds(done.shape[0], PAIR)], last_sem)
    store.start()
    for each in (*stores, store):
        each.wait()


def by_tile(tokens):
    return tokens.reshape(1, TILES, TILE, HEADS * HD)


def on_device(queries, keys, values, neighbours, w_out):
    bf16, f32 = jnp.bfloat16, jnp.float32
    dma = pltpu.SemaphoreType.DMA
    vmem = pltpu.VMEM
    width = w_out.shape[1] // 2
    done, last_rows, w_half = pl.pallas_call(
        kernel,
        out_shape=(
            vmem((ROWS - PAIR, width), bf16),
            vmem((PAIR, HEADS * HD), bf16),
            vmem((HEADS * HD, width), bf16),
        ),
        in_specs=[pl.BlockSpec(memory_space=pl.ANY)] * 5,
        out_specs=[pl.BlockSpec(memory_space=vmem)] * 3,
        scratch_shapes=[
            vmem((ROUNDS, SEQ, PAIR, HD), bf16),
            vmem((SEQ * TILES, TILE, HD), bf16),
            vmem((SEQ * TILES, TILE, HD), bf16),
            vmem((ROUNDS, 2, SEQ, TILE, HD), bf16),
            vmem((ROUNDS, SEQ, TILE, HD), bf16),
            vmem((ROUNDS, SEQ, TILE, HD), bf16),
            vmem((ROWS, HEADS * HD), bf16),
            vmem((SPAN, PAIR), f32),
            vmem((SPAN, PAIR), f32),
            vmem((SPAN, PAIR), bf16),
            vmem((SPAN, PAIR), bf16),
            pltpu.SMEM((NB, SEQ * TILES), jnp.int32), dma, dma,
            dma, dma, dma, dma,
            dma, dma((ROUNDS + 1,)),
            dma, dma((ROUNDS,)),
            dma, dma((ROUNDS,)),
            dma, dma((ROUNDS,)),
        ],
        compiler_params=pltpu.CompilerParams(
            collective_id=0, has_side_effects=True, vmem_limit_bytes=50 * 2**20
        ),
        cost_estimate=pl.CostEstimate(
            flops=11_000_000_000, bytes_accessed=20 * 2**20, transcendentals=8_700_000
        ),
    )(neighbours.T, queries, by_tile(keys), by_tile(values), w_out)
    return pl.pallas_call(
        finish_kernel,
        out_shape=jax.ShapeDtypeStruct((ROWS, width), bf16),
        in_specs=[pl.BlockSpec(memory_space=vmem)] * 3,
        out_specs=pl.BlockSpec(memory_space=pl.ANY),
        scratch_shapes=[vmem((PAIR, width), bf16), dma((STORES,)), dma],
        compiler_params=pltpu.CompilerParams(vmem_limit_bytes=40 * 2**20),
    )(done, last_rows, w_half)


def solution(mesh):
    return jax.shard_map(
        on_device,
        mesh=mesh,
        in_specs=(
            P("cfg", ("batch", "seq"), None),
            P("cfg", ("batch", "seq"), None),
            P("cfg", ("batch", "seq"), None),
            P("batch", None),
            P(),
        ),
        out_specs=P(("batch", "seq"), "cfg"),
        check_vma=False,
    )
```

```python
import jax
import jax.numpy as jnp
import numpy as np
from jax import lax
from jax.experimental import pallas as pl
from jax.experimental.pallas import tpu as pltpu
from jax.sharding import PartitionSpec as P

HEADS = 16
HD = 128
TILE = 64
GUIDANCE = 5.0
MESH = pl.DeviceIdType.MESH

SEQ = 16
RING = 4
NB = 11
ROWS = 768
ROUNDS = 6
TILES = ROWS // TILE
MIXED = (
    (1, 2), (3, 0), (0, 1), (2, 3), (3, 2), (1, 0), (0, 3), (2, 1),
    (2, 2), (1, 1), (3, 3), (0, 2), (2, 0), (1, 3), (3, 1),
)
BLK = 2
NEAR = 9
STORES = 4
COLS = 512
PAIR = 2 * TILE
PAIRS = ROUNDS * SEQ
SPAN = NB * TILE
EXP_SCALE = float(np.log2(np.e) / HD**0.5)

OFFSETS = (
    (0, 1), (0, 3), (1, 0), (3, 0),
    (1, 1), (3, 3), (1, 3), (3, 1),
    (0, 2), (2, 0),
    (1, 2), (3, 2), (2, 1), (2, 3),
    (2, 2),
)


def kernel(
    ids_hbm, q_hbm, k_hbm, v_hbm, w_hbm, out_ref, last_ref, w_buf,
    q_buf, k_buf, v_buf, att, swapped, folded, gathered,
    s_even, s_odd, p_even, p_odd,
    ids, ids_sem, w_sem, k_send, k_recv, v_send, v_recv, q_send, q_recv,
    x_send, x_recv, g_send, g_recv, f_send, f_recv,
):
    core = lax.axis_index("cfg")
    me = lax.axis_index("seq")
    z, y = me // RING, me % RING
    other_core = {"cfg": 1 - core}
    peers = [lax.rem(z + dz, RING) * RING + lax.rem(y + dy, RING) for dz, dy in OFFSETS]

    def await_bytes(ref, sem):
        pltpu.make_async_copy(ref, ref, sem).wait()

    mixed = [lax.rem(z + dz, RING) * RING + lax.rem(y + dy, RING) for dz, dy in MIXED]

    barrier = pltpu.get_barrier_semaphore()
    for peer in peers:
        pl.semaphore_signal(barrier, inc=1, device_id={"seq": peer}, device_id_type=MESH)
    pl.semaphore_signal(barrier, inc=1, device_id=other_core, device_id_type=MESH)
    pl.semaphore_wait(barrier, SEQ)

    def head_cols(head):
        return pl.ds(pl.multiple_of(head * HD, HD), HD)

    def scatter(src, buf, send, recv):
        tiles = pl.ds(me * TILES, TILES)

        def block(n, _):
            for peer in mixed:
                pltpu.make_async_remote_copy(
                    src_ref=src.at[0, pl.ds(n * BLK, BLK), :, head_cols(peer)],
                    dst_ref=buf.at[pl.ds(me * TILES + n * BLK, BLK)],
                    send_sem=send,
                    recv_sem=recv,
                    device_id={"seq": peer},
                    device_id_type=MESH,
                ).start()
            return 0

        lax.fori_loop(0, TILES // BLK, block, 0)
        pltpu.make_async_copy(src.at[0, :, :, head_cols(me)], buf.at[tiles], recv).start()

    def scatter_queries(r, recv_of):
        rows = pl.ds(pl.multiple_of(r * PAIR, PAIR), PAIR)
        for n, peer in enumerate(peers):
            pltpu.make_async_remote_copy(
                src_ref=q_hbm.at[0, rows, head_cols(peer)],
                dst_ref=q_buf.at[r, me],
                send_sem=q_send,
                recv_sem=recv_of(n),
                device_id={"seq": peer},
                device_id_type=MESH,
            ).start()
        pltpu.make_async_copy(
            q_hbm.at[0, rows, head_cols(me)], q_buf.at[r, me], recv_of(0)
        ).start()

    def scatter_later_queries(r, _):
        scatter_queries(r, lambda _: q_recv.at[r + 1])
        return 0

    remote_tiles = pl.ds(0, (SEQ - 1) * TILES)
    scatter(k_hbm, k_buf, k_send, k_recv)
    half_cols = w_hbm.shape[1] // 2
    w_copy = pltpu.make_async_copy(
        w_hbm.at[:, pl.ds(pl.multiple_of(core * half_cols, half_cols), half_cols)], w_buf, w_sem
    )
    w_copy.start()
    ids_copy = pltpu.make_async_copy(ids_hbm, ids, ids_sem)
    ids_copy.start()
    for ref in (s_even, s_odd, p_even, p_odd):
        ref[...] = jnp.zeros_like(ref)
    scatter(v_hbm, v_buf, v_send, v_recv)
    scatter_queries(0, lambda n: q_recv.at[n // (NEAR - 1)])
    lax.fori_loop(1, ROUNDS, scatter_later_queries, 0)
    await_bytes(k_buf.at[remote_tiles], k_send)
    await_bytes(v_buf.at[remote_tiles], v_send)
    await_bytes(k_buf, k_recv)
    await_bytes(v_buf, v_recv)
    w_copy.wait()
    ids_copy.wait()

    def near(buf, tile):
        return jnp.concatenate([buf[ids[j, tile]] for j in range(NB)], axis=0)

    def source(pair):
        n = pair % SEQ
        far = n // NEAR
        k = n - NEAR
        side = jnp.maximum(k, 0) // RING
        dz = (1 - far) * (n // 3 - 1) + far * ((1 - side) * 2 + side * (k - RING - 1))
        dy = (1 - far) * (n % 3 - 1) + far * ((1 - side) * k + side * 2)
        return (z + dz + RING) % RING * RING + (y + dy + RING) % RING

    def near_pair(buf, pair):
        tile = source(pair) * TILES + (pair // SEQ) * 2
        return jnp.concatenate([near(buf, tile), near(buf, tile + 1)], axis=1)

    def step(i, scores_in, scores_out, probs_in, probs_out):
        done = jnp.maximum(i - 2, 0)
        result = lax.dot_general(
            probs_in[...], near_pair(v_buf, done), (((0,), (0,)), ((), ())),
            preferred_element_type=jnp.float32,
        )
        att[done // SEQ, 0, source(done)] = result[:TILE, :HD].astype(jnp.bfloat16)
        att[done // SEQ, 1, source(done)] = result[TILE:, HD:].astype(jnp.bfloat16)
        scores = scores_in[...]
        peak = jnp.max(scores, axis=0, keepdims=True) * EXP_SCALE
        expval = jnp.exp2(scores * EXP_SCALE - peak)
        total = jnp.sum(expval, axis=0, keepdims=True)
        probs_out[...] = (expval * (1.0 / total)).astype(jnp.bfloat16)
        pair = jnp.minimum(i, PAIRS - 1)
        queries = q_buf[pair // SEQ, source(pair)]
        zero = jnp.zeros((TILE, HD), jnp.bfloat16)
        blocks = jnp.concatenate(
            [
                jnp.concatenate([queries[:TILE], zero], axis=1),
                jnp.concatenate([zero, queries[TILE:]], axis=1),
            ],
            axis=0,
        )
        scores_out[...] = lax.dot_general(
            near_pair(k_buf, pair), blocks, (((1,), (1,)), ((), ())),
            preferred_element_type=jnp.float32,
        )

    def steps(first, count):
        def two(n, _):
            i = first + 2 * n
            step(i, s_odd, s_even, p_even, p_odd)
            step(i + 1, s_even, s_odd, p_odd, p_even)
            return 0

        lax.fori_loop(0, count // 2, two, 0)

    def swap(r):
        return pltpu.make_async_remote_copy(
            src_ref=att.at[r, 1 - core],
            dst_ref=swapped.at[r],
            send_sem=x_send,
            recv_sem=x_recv.at[r],
            device_id=other_core,
            device_id_type=MESH,
        )

    own_gain = jnp.where(core == 0, GUIDANCE, 1.0 - GUIDANCE).astype(jnp.float32)
    other_gain = 1.0 - own_gain

    def round_rows(r, half):
        return pl.ds(pl.multiple_of(r * PAIR + half * TILE, TILE), TILE)

    def fold(r):
        await_bytes(swapped.at[r], x_recv.at[r])

        def some(n, _):
            part = pl.ds(n * 4, 4)
            own = att[r, core, part].astype(jnp.float32)
            other = swapped[r, part].astype(jnp.float32)
            folded[r, part] = (own * own_gain + other * other_gain).astype(jnp.bfloat16)
            return 0

        lax.fori_loop(0, SEQ // 4, some, 0)
        rows = round_rows(r, core)
        for peer in peers:
            pltpu.make_async_remote_copy(
                src_ref=folded.at[r, peer],
                dst_ref=gathered.at[rows, head_cols(me)],
                send_sem=g_send,
                recv_sem=g_recv.at[r],
                device_id={"seq": peer},
                device_id_type=MESH,
            ).start()
        pltpu.make_async_copy(
            folded.at[r, me], gathered.at[rows, head_cols(me)], g_recv.at[r]
        ).start()

    def forward(r):
        rows = round_rows(r, core)
        await_bytes(gathered.at[rows], g_recv.at[r])
        pltpu.make_async_remote_copy(
            src_ref=gathered.at[rows],
            dst_ref=gathered.at[rows],
            send_sem=f_send,
            recv_sem=f_recv.at[r],
            device_id=other_core,
            device_id_type=MESH,
        ).start()

    def project(r, rounds, first, count):
        rows = pl.ds(pl.multiple_of(r * PAIR, PAIR), rounds * PAIR)

        def columns(n, _):
            cols = pl.ds(pl.multiple_of(n * COLS, COLS), COLS)
            out_ref[rows, cols] = jnp.dot(
                gathered[rows, :], w_buf[:, cols], preferred_element_type=jnp.float32
            ).astype(jnp.bfloat16)
            return 0

        lax.fori_loop(first, first + count, columns, 0)

    def await_forward(r):
        await_bytes(gathered.at[round_rows(r, 1 - core)], f_recv.at[r])

    def one_round(r, _):
        await_bytes(q_buf.at[r], q_recv.at[r + 1])
        steps(r * SEQ, 2)
        swap(r - 1).start()
        steps(r * SEQ + 2, 8)
        fold(r - 1)
        steps(r * SEQ + 10, 6)
        return 0

    await_bytes(q_buf.at[0, pl.ds(0, NEAR)], q_recv.at[0])
    steps(0, NEAR - 1)
    await_bytes(q_buf.at[0, pl.ds(0, SEQ - NEAR)], q_recv.at[1])
    steps(NEAR - 1, SEQ - NEAR + 1)
    lax.fori_loop(1, ROUNDS, one_round, 0)
    steps(PAIRS, 2)
    last = ROUNDS - 1
    swap(last).start()
    forward(0)
    forward(1)
    fold(last)
    blocks = half_cols // COLS
    forward(2)
    await_forward(0)
    await_forward(1)
    project(0, 2, 0, 4)
    forward(3)
    await_forward(2)
    project(2, 1, 0, 4)
    forward(4)
    await_forward(3)
    project(3, 1, 0, 4)
    forward(5)
    await_forward(4)
    project(4, 1, 0, 4)
    await_forward(5)
    last_ref[...] = gathered[pl.ds(last * PAIR, PAIR), :]

    await_bytes(q_buf.at[:, pl.ds(0, SEQ - 1)], q_send)
    await_bytes(swapped, x_send)
    await_bytes(folded.at[:, pl.ds(0, SEQ - 1)], g_send)
    await_bytes(swapped, f_send)


def finish_kernel(done, last_rows, w_half, out_hbm, last_out, sems, last_sem):
    size = done.shape[0] // STORES
    stores = [
        pltpu.make_async_copy(
            done.at[pl.ds(n * size, size)], out_hbm.at[pl.ds(n * size, size)], sems.at[n]
        )
        for n in range(STORES)
    ]
    for store in stores:
        store.start()
    step = 512
    for n in range(last_out.shape[1] // step):
        cols = pl.ds(n * step, step)
        last_out[:, cols] = jnp.dot(
            last_rows[...], w_half[:, cols], preferred_element_type=jnp.float32
        ).astype(jnp.bfloat16)
    store = pltpu.make_async_copy(last_out, out_hbm.at[pl.ds(done.shape[0], PAIR)], last_sem)
    store.start()
    for each in (*stores, store):
        each.wait()


def by_tile(tokens):
    return tokens.reshape(1, TILES, TILE, HEADS * HD)


def on_device(queries, keys, values, neighbours, w_out):
    bf16, f32 = jnp.bfloat16, jnp.float32
    dma = pltpu.SemaphoreType.DMA
    vmem = pltpu.VMEM
    width = w_out.shape[1] // 2
    done, last_rows, w_half = pl.pallas_call(
        kernel,
        out_shape=(
            vmem((ROWS - PAIR, width), bf16),
            vmem((PAIR, HEADS * HD), bf16),
            vmem((HEADS * HD, width), bf16),
        ),
        in_specs=[pl.BlockSpec(memory_space=pl.ANY)] * 5,
        out_specs=[pl.BlockSpec(memory_space=vmem)] * 3,
        scratch_shapes=[
            vmem((ROUNDS, SEQ, PAIR, HD), bf16),
            vmem((SEQ * TILES, TILE, HD), bf16),
            vmem((SEQ * TILES, TILE, HD), bf16),
            vmem((ROUNDS, 2, SEQ, TILE, HD), bf16),
            vmem((ROUNDS, SEQ, TILE, HD), bf16),
            vmem((ROUNDS, SEQ, TILE, HD), bf16),
            vmem((ROWS, HEADS * HD), bf16),
            vmem((SPAN, PAIR), f32),
            vmem((SPAN, PAIR), f32),
            vmem((SPAN, PAIR), bf16),
            vmem((SPAN, PAIR), bf16),
            pltpu.SMEM((NB, SEQ * TILES), jnp.int32), dma, dma,
            dma, dma, dma, dma,
            dma, dma((ROUNDS + 1,)),
            dma, dma((ROUNDS,)),
            dma, dma((ROUNDS,)),
            dma, dma((ROUNDS,)),
        ],
        compiler_params=pltpu.CompilerParams(
            collective_id=0, has_side_effects=True, vmem_limit_bytes=50 * 2**20
        ),
        cost_estimate=pl.CostEstimate(
            flops=11_000_000_000, bytes_accessed=20 * 2**20, transcendentals=8_700_000
        ),
    )(neighbours.T, queries, by_tile(keys), by_tile(values), w_out)
    return pl.pallas_call(
        finish_kernel,
        out_shape=jax.ShapeDtypeStruct((ROWS, width), bf16),
        in_specs=[pl.BlockSpec(memory_space=vmem)] * 3,
        out_specs=pl.BlockSpec(memory_space=pl.ANY),
        scratch_shapes=[vmem((PAIR, width), bf16), dma((STORES,)), dma],
        compiler_params=pltpu.CompilerParams(vmem_limit_bytes=40 * 2**20),
    )(done, last_rows, w_half)


def solution(mesh):
    return jax.shard_map(
        on_device,
        mesh=mesh,
        in_specs=(
            P("cfg", ("batch", "seq"), None),
            P("cfg", ("batch", "seq"), None),
            P("cfg", ("batch", "seq"), None),
            P("batch", None),
            P(),
        ),
        out_specs=P(("batch", "seq"), "cfg"),
        check_vma=False,
    )
```

```python
import jax
import jax.numpy as jnp
import numpy as np
from jax import lax
from jax.experimental import pallas as pl
from jax.experimental.pallas import tpu as pltpu
from jax.sharding import PartitionSpec as P

HEADS = 16
HD = 128
TILE = 64
GUIDANCE = 5.0
MESH = pl.DeviceIdType.MESH

SEQ = 16
RING = 4
NB = 11
ROWS = 768
ROUNDS = 6
TILES = ROWS // TILE
MIXED = (
    (1, 2), (3, 0), (0, 1), (2, 3), (3, 2), (1, 0), (0, 3), (2, 1),
    (2, 2), (1, 1), (3, 3), (0, 2), (2, 0), (1, 3), (3, 1),
)
BLK = 2
NEAR = 9
STORES = 4
COLS = 512
PAIR = 2 * TILE
PAIRS = ROUNDS * SEQ
SPAN = NB * TILE
EXP_SCALE = float(np.log2(np.e) / HD**0.5)

OFFSETS = (
    (0, 1), (0, 3), (1, 0), (3, 0),
    (1, 1), (3, 3), (1, 3), (3, 1),
    (0, 2), (2, 0),
    (1, 2), (3, 2), (2, 1), (2, 3),
    (2, 2),
)


def kernel(
    ids_hbm, q_hbm, k_hbm, v_hbm, w_hbm, out_ref, last_ref, w_buf,
    q_buf, k_buf, v_buf, att, swapped, folded, gathered,
    s_even, s_odd, p_even, p_odd,
    ids, ids_sem, w_sem, k_send, k_recv, v_send, v_recv, q_send, q_recv,
    x_send, x_recv, g_send, g_recv, f_send, f_recv,
):
    core = lax.axis_index("cfg")
    me = lax.axis_index("seq")
    z, y = me // RING, me % RING
    other_core = {"cfg": 1 - core}
    peers = [lax.rem(z + dz, RING) * RING + lax.rem(y + dy, RING) for dz, dy in OFFSETS]

    def await_bytes(ref, sem):
        pltpu.make_async_copy(ref, ref, sem).wait()

    mixed = [lax.rem(z + dz, RING) * RING + lax.rem(y + dy, RING) for dz, dy in MIXED]

    barrier = pltpu.get_barrier_semaphore()
    for peer in peers:
        pl.semaphore_signal(barrier, inc=1, device_id={"seq": peer}, device_id_type=MESH)
    pl.semaphore_signal(barrier, inc=1, device_id=other_core, device_id_type=MESH)
    pl.semaphore_wait(barrier, SEQ)

    def head_cols(head):
        return pl.ds(pl.multiple_of(head * HD, HD), HD)

    def scatter(src, buf, send, recv):
        tiles = pl.ds(me * TILES, TILES)

        def block(n, _):
            for peer in mixed:
                pltpu.make_async_remote_copy(
                    src_ref=src.at[0, pl.ds(n * BLK, BLK), :, head_cols(peer)],
                    dst_ref=buf.at[pl.ds(me * TILES + n * BLK, BLK)],
                    send_sem=send,
                    recv_sem=recv,
                    device_id={"seq": peer},
                    device_id_type=MESH,
                ).start()
            return 0

        lax.fori_loop(0, TILES // BLK, block, 0)
        pltpu.make_async_copy(src.at[0, :, :, head_cols(me)], buf.at[tiles], recv).start()

    def scatter_queries(r, recv_of):
        rows = pl.ds(pl.multiple_of(r * PAIR, PAIR), PAIR)
        for n, peer in enumerate(peers):
            pltpu.make_async_remote_copy(
                src_ref=q_hbm.at[0, rows, head_cols(peer)],
                dst_ref=q_buf.at[r, me],
                send_sem=q_send,
                recv_sem=recv_of(n),
                device_id={"seq": peer},
                device_id_type=MESH,
            ).start()
        pltpu.make_async_copy(
            q_hbm.at[0, rows, head_cols(me)], q_buf.at[r, me], recv_of(0)
        ).start()

    def scatter_later_queries(r, _):
        scatter_queries(r, lambda _: q_recv.at[r + 1])
        return 0

    remote_tiles = pl.ds(0, (SEQ - 1) * TILES)
    scatter(k_hbm, k_buf, k_send, k_recv)
    half_cols = w_hbm.shape[1] // 2
    w_copy = pltpu.make_async_copy(
        w_hbm.at[:, pl.ds(pl.multiple_of(core * half_cols, half_cols), half_cols)], w_buf, w_sem
    )
    w_copy.start()
    ids_copy = pltpu.make_async_copy(ids_hbm, ids, ids_sem)
    ids_copy.start()
    for ref in (s_even, s_odd, p_even, p_odd):
        ref[...] = jnp.zeros_like(ref)
    scatter(v_hbm, v_buf, v_send, v_recv)
    scatter_queries(0, lambda n: q_recv.at[n // (NEAR - 1)])
    lax.fori_loop(1, ROUNDS, scatter_later_queries, 0)
    await_bytes(k_buf.at[remote_tiles], k_send)
    await_bytes(v_buf.at[remote_tiles], v_send)
    await_bytes(k_buf, k_recv)
    await_bytes(v_buf, v_recv)
    w_copy.wait()
    ids_copy.wait()

    def near(buf, tile):
        return jnp.concatenate([buf[ids[j, tile]] for j in range(NB)], axis=0)

    def source(pair):
        n = pair % SEQ
        far = n // NEAR
        k = n - NEAR
        side = jnp.maximum(k, 0) // RING
        dz = (1 - far) * (n // 3 - 1) + far * ((1 - side) * 2 + side * (k - RING - 1))
        dy = (1 - far) * (n % 3 - 1) + far * ((1 - side) * k + side * 2)
        return (z + dz + RING) % RING * RING + (y + dy + RING) % RING

    def near_pair(buf, pair):
        tile = source(pair) * TILES + (pair // SEQ) * 2
        return jnp.concatenate([near(buf, tile), near(buf, tile + 1)], axis=1)

    def step(i, scores_in, scores_out, probs_in, probs_out, left=3):
        done = jnp.maximum(i - 2, 0)
        result = lax.dot_general(
            probs_in[...], near_pair(v_buf, done), (((0,), (0,)), ((), ())),
            preferred_element_type=jnp.float32,
        )
        att[done // SEQ, 0, source(done)] = result[:TILE, :HD].astype(jnp.bfloat16)
        att[done // SEQ, 1, source(done)] = result[TILE:, HD:].astype(jnp.bfloat16)
        if left == 1:
            return
        scores = scores_in[...]
        peak = jnp.max(scores, axis=0, keepdims=True) * EXP_SCALE
        expval = jnp.exp2(scores * EXP_SCALE - peak)
        total = jnp.sum(expval, axis=0, keepdims=True)
        probs_out[...] = (expval * (1.0 / total)).astype(jnp.bfloat16)
        if left == 2:
            return
        pair = jnp.minimum(i, PAIRS - 1)
        queries = q_buf[pair // SEQ, source(pair)]
        zero = jnp.zeros((TILE, HD), jnp.bfloat16)
        blocks = jnp.concatenate(
            [
                jnp.concatenate([queries[:TILE], zero], axis=1),
                jnp.concatenate([zero, queries[TILE:]], axis=1),
            ],
            axis=0,
        )
        scores_out[...] = lax.dot_general(
            near_pair(k_buf, pair), blocks, (((1,), (1,)), ((), ())),
            preferred_element_type=jnp.float32,
        )

    def steps(first, count):
        def two(n, _):
            i = first + 2 * n
            step(i, s_odd, s_even, p_even, p_odd)
            step(i + 1, s_even, s_odd, p_odd, p_even)
            return 0

        lax.fori_loop(0, count // 2, two, 0)

    def swap(r):
        return pltpu.make_async_remote_copy(
            src_ref=att.at[r, 1 - core],
            dst_ref=swapped.at[r],
            send_sem=x_send,
            recv_sem=x_recv.at[r],
            device_id=other_core,
            device_id_type=MESH,
        )

    own_gain = jnp.where(core == 0, GUIDANCE, 1.0 - GUIDANCE).astype(jnp.float32)
    other_gain = 1.0 - own_gain

    def round_rows(r, half):
        return pl.ds(pl.multiple_of(r * PAIR + half * TILE, TILE), TILE)

    def fold(r):
        await_bytes(swapped.at[r], x_recv.at[r])

        def some(n, _):
            part = pl.ds(n * 4, 4)
            own = att[r, core, part].astype(jnp.float32)
            other = swapped[r, part].astype(jnp.float32)
            folded[r, part] = (own * own_gain + other * other_gain).astype(jnp.bfloat16)
            return 0

        lax.fori_loop(0, SEQ // 4, some, 0)
        rows = round_rows(r, core)
        for peer in peers:
            pltpu.make_async_remote_copy(
                src_ref=folded.at[r, peer],
                dst_ref=gathered.at[rows, head_cols(me)],
                send_sem=g_send,
                recv_sem=g_recv.at[r],
                device_id={"seq": peer},
                device_id_type=MESH,
            ).start()
        pltpu.make_async_copy(
            folded.at[r, me], gathered.at[rows, head_cols(me)], g_recv.at[r]
        ).start()

    def forward(r):
        rows = round_rows(r, core)
        await_bytes(gathered.at[rows], g_recv.at[r])
        pltpu.make_async_remote_copy(
            src_ref=gathered.at[rows],
            dst_ref=gathered.at[rows],
            send_sem=f_send,
            recv_sem=f_recv.at[r],
            device_id=other_core,
            device_id_type=MESH,
        ).start()

    def project(r, rounds, first, count):
        rows = pl.ds(pl.multiple_of(r * PAIR, PAIR), rounds * PAIR)

        def columns(n, _):
            cols = pl.ds(pl.multiple_of(n * COLS, COLS), COLS)
            out_ref[rows, cols] = jnp.dot(
                gathered[rows, :], w_buf[:, cols], preferred_element_type=jnp.float32
            ).astype(jnp.bfloat16)
            return 0

        lax.fori_loop(first, first + count, columns, 0)

    def await_forward(r):
        await_bytes(gathered.at[round_rows(r, 1 - core)], f_recv.at[r])

    def one_round(r, _):
        await_bytes(q_buf.at[r], q_recv.at[r + 1])
        steps(r * SEQ, 2)
        swap(r - 1).start()
        steps(r * SEQ + 2, 8)
        fold(r - 1)
        steps(r * SEQ + 10, 6)
        return 0

    await_bytes(q_buf.at[0, pl.ds(0, NEAR)], q_recv.at[0])
    steps(0, NEAR - 1)
    await_bytes(q_buf.at[0, pl.ds(0, SEQ - NEAR)], q_recv.at[1])
    steps(NEAR - 1, SEQ - NEAR + 1)
    lax.fori_loop(1, ROUNDS, one_round, 0)
    step(PAIRS, s_odd, s_even, p_even, p_odd, 2)
    step(PAIRS + 1, s_even, s_odd, p_odd, p_even, 1)
    last = ROUNDS - 1
    swap(last).start()
    forward(0)
    forward(1)
    fold(last)
    blocks = half_cols // COLS
    forward(2)
    await_forward(0)
    await_forward(1)
    project(0, 2, 0, 4)
    forward(3)
    await_forward(2)
    project(2, 1, 0, 4)
    forward(4)
    await_forward(3)
    project(3, 1, 0, 4)
    forward(5)
    await_forward(4)
    project(4, 1, 0, 4)
    await_forward(5)
    last_ref[...] = gathered[pl.ds(last * PAIR, PAIR), :]

    await_bytes(q_buf.at[:, pl.ds(0, SEQ - 1)], q_send)
    await_bytes(swapped, x_send)
    await_bytes(folded.at[:, pl.ds(0, SEQ - 1)], g_send)
    await_bytes(swapped, f_send)


def finish_kernel(done, last_rows, w_half, out_hbm, last_out, sems, last_sem):
    size = done.shape[0] // STORES
    stores = [
        pltpu.make_async_copy(
            done.at[pl.ds(n * size, size)], out_hbm.at[pl.ds(n * size, size)], sems.at[n]
        )
        for n in range(STORES)
    ]
    for store in stores:
        store.start()
    step = 512
    for n in range(last_out.shape[1] // step):
        cols = pl.ds(n * step, step)
        last_out[:, cols] = jnp.dot(
            last_rows[...], w_half[:, cols], preferred_element_type=jnp.float32
        ).astype(jnp.bfloat16)
    store = pltpu.make_async_copy(last_out, out_hbm.at[pl.ds(done.shape[0], PAIR)], last_sem)
    store.start()
    for each in (*stores, store):
        each.wait()


def by_tile(tokens):
    return tokens.reshape(1, TILES, TILE, HEADS * HD)


def on_device(queries, keys, values, neighbours, w_out):
    bf16, f32 = jnp.bfloat16, jnp.float32
    dma = pltpu.SemaphoreType.DMA
    vmem = pltpu.VMEM
    width = w_out.shape[1] // 2
    done, last_rows, w_half = pl.pallas_call(
        kernel,
        out_shape=(
            vmem((ROWS - PAIR, width), bf16),
            vmem((PAIR, HEADS * HD), bf16),
            vmem((HEADS * HD, width), bf16),
        ),
        in_specs=[pl.BlockSpec(memory_space=pl.ANY)] * 5,
        out_specs=[pl.BlockSpec(memory_space=vmem)] * 3,
        scratch_shapes=[
            vmem((ROUNDS, SEQ, PAIR, HD), bf16),
            vmem((SEQ * TILES, TILE, HD), bf16),
            vmem((SEQ * TILES, TILE, HD), bf16),
            vmem((ROUNDS, 2, SEQ, TILE, HD), bf16),
            vmem((ROUNDS, SEQ, TILE, HD), bf16),
            vmem((ROUNDS, SEQ, TILE, HD), bf16),
            vmem((ROWS, HEADS * HD), bf16),
            vmem((SPAN, PAIR), f32),
            vmem((SPAN, PAIR), f32),
            vmem((SPAN, PAIR), bf16),
            vmem((SPAN, PAIR), bf16),
            pltpu.SMEM((NB, SEQ * TILES), jnp.int32), dma, dma,
            dma, dma, dma, dma,
            dma, dma((ROUNDS + 1,)),
            dma, dma((ROUNDS,)),
            dma, dma((ROUNDS,)),
            dma, dma((ROUNDS,)),
        ],
        compiler_params=pltpu.CompilerParams(
            collective_id=0, has_side_effects=True, vmem_limit_bytes=50 * 2**20
        ),
        cost_estimate=pl.CostEstimate(
            flops=11_000_000_000, bytes_accessed=20 * 2**20, transcendentals=8_700_000
        ),
    )(neighbours.T, queries, by_tile(keys), by_tile(values), w_out)
    return pl.pallas_call(
        finish_kernel,
        out_shape=jax.ShapeDtypeStruct((ROWS, width), bf16),
        in_specs=[pl.BlockSpec(memory_space=vmem)] * 3,
        out_specs=pl.BlockSpec(memory_space=pl.ANY),
        scratch_shapes=[vmem((PAIR, width), bf16), dma((STORES,)), dma],
        compiler_params=pltpu.CompilerParams(vmem_limit_bytes=40 * 2**20),
    )(done, last_rows, w_half)


def solution(mesh):
    return jax.shard_map(
        on_device,
        mesh=mesh,
        in_specs=(
            P("cfg", ("batch", "seq"), None),
            P("cfg", ("batch", "seq"), None),
            P("cfg", ("batch", "seq"), None),
            P("batch", None),
            P(),
        ),
        out_specs=P(("batch", "seq"), "cfg"),
        check_vma=False,
    )
```

```python
import jax
import jax.numpy as jnp
import numpy as np
from jax import lax
from jax.experimental import pallas as pl
from jax.experimental.pallas import tpu as pltpu
from jax.sharding import PartitionSpec as P

HEADS = 16
HD = 128
TILE = 64
GUIDANCE = 5.0
MESH = pl.DeviceIdType.MESH

SEQ = 16
RING = 4
NB = 11
ROWS = 768
ROUNDS = 6
TILES = ROWS // TILE
MIXED = (
    (1, 2), (3, 0), (0, 1), (2, 3), (3, 2), (1, 0), (0, 3), (2, 1),
    (2, 2), (1, 1), (3, 3), (0, 2), (2, 0), (1, 3), (3, 1),
)
BLK = 1
NEAR = 9
STORES = 4
COLS = 512
PAIR = 2 * TILE
PAIRS = ROUNDS * SEQ
SPAN = NB * TILE
EXP_SCALE = float(np.log2(np.e) / HD**0.5)

OFFSETS = (
    (0, 1), (0, 3), (1, 0), (3, 0),
    (1, 1), (3, 3), (1, 3), (3, 1),
    (0, 2), (2, 0),
    (1, 2), (3, 2), (2, 1), (2, 3),
    (2, 2),
)


def kernel(
    ids_hbm, q_hbm, k_hbm, v_hbm, w_hbm, out_ref, last_ref, w_buf,
    q_buf, k_buf, v_buf, att, swapped, folded, gathered,
    s_even, s_odd, p_even, p_odd,
    ids, ids_sem, w_sem, k_send, k_recv, v_send, v_recv, q_send, q_recv,
    x_send, x_recv, g_send, g_recv, f_send, f_recv,
):
    core = lax.axis_index("cfg")
    me = lax.axis_index("seq")
    z, y = me // RING, me % RING
    other_core = {"cfg": 1 - core}
    peers = [lax.rem(z + dz, RING) * RING + lax.rem(y + dy, RING) for dz, dy in OFFSETS]

    def await_bytes(ref, sem):
        pltpu.make_async_copy(ref, ref, sem).wait()

    mixed = [lax.rem(z + dz, RING) * RING + lax.rem(y + dy, RING) for dz, dy in MIXED]

    barrier = pltpu.get_barrier_semaphore()
    for peer in peers:
        pl.semaphore_signal(barrier, inc=1, device_id={"seq": peer}, device_id_type=MESH)
    pl.semaphore_signal(barrier, inc=1, device_id=other_core, device_id_type=MESH)
    pl.semaphore_wait(barrier, SEQ)

    def head_cols(head):
        return pl.ds(pl.multiple_of(head * HD, HD), HD)

    def scatter(src, buf, send, recv):
        tiles = pl.ds(me * TILES, TILES)

        def block(n, _):
            for peer in mixed:
                pltpu.make_async_remote_copy(
                    src_ref=src.at[0, pl.ds(n * BLK, BLK), :, head_cols(peer)],
                    dst_ref=buf.at[pl.ds(me * TILES + n * BLK, BLK)],
                    send_sem=send,
                    recv_sem=recv,
                    device_id={"seq": peer},
                    device_id_type=MESH,
                ).start()
            return 0

        lax.fori_loop(0, TILES // BLK, block, 0)
        pltpu.make_async_copy(src.at[0, :, :, head_cols(me)], buf.at[tiles], recv).start()

    def scatter_queries(r, recv_of):
        rows = pl.ds(pl.multiple_of(r * PAIR, PAIR), PAIR)
        for n, peer in enumerate(peers):
            pltpu.make_async_remote_copy(
                src_ref=q_hbm.at[0, rows, head_cols(peer)],
                dst_ref=q_buf.at[r, me],
                send_sem=q_send,
                recv_sem=recv_of(n),
                device_id={"seq": peer},
                device_id_type=MESH,
            ).start()
        pltpu.make_async_copy(
            q_hbm.at[0, rows, head_cols(me)], q_buf.at[r, me], recv_of(0)
        ).start()

    def scatter_later_queries(r, _):
        scatter_queries(r, lambda _: q_recv.at[r + 1])
        return 0

    remote_tiles = pl.ds(0, (SEQ - 1) * TILES)
    scatter(k_hbm, k_buf, k_send, k_recv)
    half_cols = w_hbm.shape[1] // 2
    w_copy = pltpu.make_async_copy(
        w_hbm.at[:, pl.ds(pl.multiple_of(core * half_cols, half_cols), half_cols)], w_buf, w_sem
    )
    w_copy.start()
    ids_copy = pltpu.make_async_copy(ids_hbm, ids, ids_sem)
    ids_copy.start()
    for ref in (s_even, s_odd, p_even, p_odd):
        ref[...] = jnp.zeros_like(ref)
    scatter(v_hbm, v_buf, v_send, v_recv)
    scatter_queries(0, lambda n: q_recv.at[n // (NEAR - 1)])
    lax.fori_loop(1, ROUNDS, scatter_later_queries, 0)
    await_bytes(k_buf.at[remote_tiles], k_send)
    await_bytes(v_buf.at[remote_tiles], v_send)
    await_bytes(k_buf, k_recv)
    await_bytes(v_buf, v_recv)
    w_copy.wait()
    ids_copy.wait()

    def near(buf, tile):
        return jnp.concatenate([buf[ids[j, tile]] for j in range(NB)], axis=0)

    def source(pair):
        n = pair % SEQ
        far = n // NEAR
        k = n - NEAR
        side = jnp.maximum(k, 0) // RING
        dz = (1 - far) * (n // 3 - 1) + far * ((1 - side) * 2 + side * (k - RING - 1))
        dy = (1 - far) * (n % 3 - 1) + far * ((1 - side) * k + side * 2)
        return (z + dz + RING) % RING * RING + (y + dy + RING) % RING

    def near_pair(buf, pair):
        tile = source(pair) * TILES + (pair // SEQ) * 2
        return jnp.concatenate([near(buf, tile), near(buf, tile + 1)], axis=1)

    def step(i, scores_in, scores_out, probs_in, probs_out):
        done = jnp.maximum(i - 2, 0)
        result = lax.dot_general(
            probs_in[...], near_pair(v_buf, done), (((0,), (0,)), ((), ())),
            preferred_element_type=jnp.float32,
        )
        att[done // SEQ, 0, source(done)] = result[:TILE, :HD].astype(jnp.bfloat16)
        att[done // SEQ, 1, source(done)] = result[TILE:, HD:].astype(jnp.bfloat16)
        scores = scores_in[...]
        peak = jnp.max(scores, axis=0, keepdims=True) * EXP_SCALE
        expval = jnp.exp2(scores * EXP_SCALE - peak)
        total = jnp.sum(expval, axis=0, keepdims=True)
        probs_out[...] = (expval * (1.0 / total)).astype(jnp.bfloat16)
        pair = jnp.minimum(i, PAIRS - 1)
        queries = q_buf[pair // SEQ, source(pair)]
        zero = jnp.zeros((TILE, HD), jnp.bfloat16)
        blocks = jnp.concatenate(
            [
                jnp.concatenate([queries[:TILE], zero], axis=1),
                jnp.concatenate([zero, queries[TILE:]], axis=1),
            ],
            axis=0,
        )
        scores_out[...] = lax.dot_general(
            near_pair(k_buf, pair), blocks, (((1,), (1,)), ((), ())),
            preferred_element_type=jnp.float32,
        )

    def steps(first, count):
        def two(n, _):
            i = first + 2 * n
            step(i, s_odd, s_even, p_even, p_odd)
            step(i + 1, s_even, s_odd, p_odd, p_even)
            return 0

        lax.fori_loop(0, count // 2, two, 0)

    def swap(r):
        return pltpu.make_async_remote_copy(
            src_ref=att.at[r, 1 - core],
            dst_ref=swapped.at[r],
            send_sem=x_send,
            recv_sem=x_recv.at[r],
            device_id=other_core,
            device_id_type=MESH,
        )

    own_gain = jnp.where(core == 0, GUIDANCE, 1.0 - GUIDANCE).astype(jnp.float32)
    other_gain = 1.0 - own_gain

    def round_rows(r, half):
        return pl.ds(pl.multiple_of(r * PAIR + half * TILE, TILE), TILE)

    def fold(r):
        await_bytes(swapped.at[r], x_recv.at[r])

        def some(n, _):
            part = pl.ds(n * 4, 4)
            own = att[r, core, part].astype(jnp.float32)
            other = swapped[r, part].astype(jnp.float32)
            folded[r, part] = (own * own_gain + other * other_gain).astype(jnp.bfloat16)
            return 0

        lax.fori_loop(0, SEQ // 4, some, 0)
        rows = round_rows(r, core)
        for peer in peers:
            pltpu.make_async_remote_copy(
                src_ref=folded.at[r, peer],
                dst_ref=gathered.at[rows, head_cols(me)],
                send_sem=g_send,
                recv_sem=g_recv.at[r],
                device_id={"seq": peer},
                device_id_type=MESH,
            ).start()
        pltpu.make_async_copy(
            folded.at[r, me], gathered.at[rows, head_cols(me)], g_recv.at[r]
        ).start()

    def forward(r):
        rows = round_rows(r, core)
        await_bytes(gathered.at[rows], g_recv.at[r])
        pltpu.make_async_remote_copy(
            src_ref=gathered.at[rows],
            dst_ref=gathered.at[rows],
            send_sem=f_send,
            recv_sem=f_recv.at[r],
            device_id=other_core,
            device_id_type=MESH,
        ).start()

    def project(r, rounds, first, count):
        rows = pl.ds(pl.multiple_of(r * PAIR, PAIR), rounds * PAIR)

        def columns(n, _):
            cols = pl.ds(pl.multiple_of(n * COLS, COLS), COLS)
            out_ref[rows, cols] = jnp.dot(
                gathered[rows, :], w_buf[:, cols], preferred_element_type=jnp.float32
            ).astype(jnp.bfloat16)
            return 0

        lax.fori_loop(first, first + count, columns, 0)

    def await_forward(r):
        await_bytes(gathered.at[round_rows(r, 1 - core)], f_recv.at[r])

    def one_round(r, _):
        await_bytes(q_buf.at[r], q_recv.at[r + 1])
        steps(r * SEQ, 2)
        swap(r - 1).start()
        steps(r * SEQ + 2, 8)
        fold(r - 1)
        steps(r * SEQ + 10, 6)
        return 0

    await_bytes(q_buf.at[0, pl.ds(0, NEAR)], q_recv.at[0])
    steps(0, NEAR - 1)
    await_bytes(q_buf.at[0, pl.ds(0, SEQ - NEAR)], q_recv.at[1])
    steps(NEAR - 1, SEQ - NEAR + 1)
    lax.fori_loop(1, ROUNDS, one_round, 0)
    steps(PAIRS, 2)
    last = ROUNDS - 1
    swap(last).start()
    forward(0)
    forward(1)
    fold(last)
    blocks = half_cols // COLS
    forward(2)
    await_forward(0)
    await_forward(1)
    project(0, 2, 0, 4)
    forward(3)
    await_forward(2)
    project(2, 1, 0, 4)
    forward(4)
    await_forward(3)
    project(3, 1, 0, 4)
    forward(5)
    await_forward(4)
    project(4, 1, 0, 4)
    await_forward(5)
    last_ref[...] = gathered[pl.ds(last * PAIR, PAIR), :]

    await_bytes(q_buf.at[:, pl.ds(0, SEQ - 1)], q_send)
    await_bytes(swapped, x_send)
    await_bytes(folded.at[:, pl.ds(0, SEQ - 1)], g_send)
    await_bytes(swapped, f_send)


def finish_kernel(done, last_rows, w_half, out_hbm, last_out, sems, last_sem):
    size = done.shape[0] // STORES
    stores = [
        pltpu.make_async_copy(
            done.at[pl.ds(n * size, size)], out_hbm.at[pl.ds(n * size, size)], sems.at[n]
        )
        for n in range(STORES)
    ]
    for store in stores:
        store.start()
    step = 512
    for n in range(last_out.shape[1] // step):
        cols = pl.ds(n * step, step)
        last_out[:, cols] = jnp.dot(
            last_rows[...], w_half[:, cols], preferred_element_type=jnp.float32
        ).astype(jnp.bfloat16)
    store = pltpu.make_async_copy(last_out, out_hbm.at[pl.ds(done.shape[0], PAIR)], last_sem)
    store.start()
    for each in (*stores, store):
        each.wait()


def by_tile(tokens):
    return tokens.reshape(1, TILES, TILE, HEADS * HD)


def on_device(queries, keys, values, neighbours, w_out):
    bf16, f32 = jnp.bfloat16, jnp.float32
    dma = pltpu.SemaphoreType.DMA
    vmem = pltpu.VMEM
    width = w_out.shape[1] // 2
    done, last_rows, w_half = pl.pallas_call(
        kernel,
        out_shape=(
            vmem((ROWS - PAIR, width), bf16),
            vmem((PAIR, HEADS * HD), bf16),
            vmem((HEADS * HD, width), bf16),
        ),
        in_specs=[pl.BlockSpec(memory_space=pl.ANY)] * 5,
        out_specs=[pl.BlockSpec(memory_space=vmem)] * 3,
        scratch_shapes=[
            vmem((ROUNDS, SEQ, PAIR, HD), bf16),
            vmem((SEQ * TILES, TILE, HD), bf16),
            vmem((SEQ * TILES, TILE, HD), bf16),
            vmem((ROUNDS, 2, SEQ, TILE, HD), bf16),
            vmem((ROUNDS, SEQ, TILE, HD), bf16),
            vmem((ROUNDS, SEQ, TILE, HD), bf16),
            vmem((ROWS, HEADS * HD), bf16),
            vmem((SPAN, PAIR), f32),
            vmem((SPAN, PAIR), f32),
            vmem((SPAN, PAIR), bf16),
            vmem((SPAN, PAIR), bf16),
            pltpu.SMEM((NB, SEQ * TILES), jnp.int32), dma, dma,
            dma, dma, dma, dma,
            dma, dma((ROUNDS + 1,)),
            dma, dma((ROUNDS,)),
            dma, dma((ROUNDS,)),
            dma, dma((ROUNDS,)),
        ],
        compiler_params=pltpu.CompilerParams(
            collective_id=0, has_side_effects=True, vmem_limit_bytes=50 * 2**20
        ),
        cost_estimate=pl.CostEstimate(
            flops=11_000_000_000, bytes_accessed=20 * 2**20, transcendentals=8_700_000
        ),
    )(neighbours.T, queries, by_tile(keys), by_tile(values), w_out)
    return pl.pallas_call(
        finish_kernel,
        out_shape=jax.ShapeDtypeStruct((ROWS, width), bf16),
        in_specs=[pl.BlockSpec(memory_space=vmem)] * 3,
        out_specs=pl.BlockSpec(memory_space=pl.ANY),
        scratch_shapes=[vmem((PAIR, width), bf16), dma((STORES,)), dma],
        compiler_params=pltpu.CompilerParams(vmem_limit_bytes=40 * 2**20),
    )(done, last_rows, w_half)


def solution(mesh):
    return jax.shard_map(
        on_device,
        mesh=mesh,
        in_specs=(
            P("cfg", ("batch", "seq"), None),
            P("cfg", ("batch", "seq"), None),
            P("cfg", ("batch", "seq"), None),
            P("batch", None),
            P(),
        ),
        out_specs=P(("batch", "seq"), "cfg"),
        check_vma=False,
    )
```
